256 devices in a mesh: grp: 8 (over z_lo, core), tm: 32 (over z_hi, y, x).
Axes of the slice: x: 4, y: 4, z: 8 (z_hi: 2, z_lo: 4; z = z_hi * 4 + z_lo), core: 2. Of those that a mesh axis runs over, the one named last changes fastest.
Arguments:
- x_start: float32 [4096, 128], P(('grp', 'tm')), may hold values from -3 to 3
- y_start: float32 [1024, 128], P('tm'), may hold values from 0 to 1
- cost: float32 [4096, 128], P(('grp', 'tm')), may hold values from -6 to 6
- rhs: float32 [1024, 128], P('tm'), may hold values from -6 to 6
- tiles: float32 [16384, 128, 128], P(('grp', 'tm')), may hold values from -0.1875 to 0.1875
- tile_rows: int32 [16384], P(('grp', 'tm')), may hold values from 0 to 1023, as said below
- tile_cols: int32 [16384], P(('grp', 'tm')), may hold values from 0 to 4095, as said below
- tile_count: int32 [256], P(('grp', 'tm')), may hold values from 1 to 64, as said below
- var_class: int32 [4096, 128], P(('grp', 'tm')), may hold values from 0 to 7
- lower_table: float32 [8], replicated, may hold values from -1 to -0.2
- upper_table: float32 [8], replicated, may hold values from 0.2 to 1
Outputs:
- primal: float32 [4096, 128], P(('grp', 'tm'))
- dual: float32 [1024, 128], P('tm')
- primal_mean: float32 [4096, 128], P(('grp', 'tm'))
- dual_mean: float32 [1024, 128], P('tm')
The draws below stay inside these ranges and needn't reach their ends.
Inputs may be any that keep to these rules, and one draw needn't show every extreme that they name: `tile_cols`: the tile slots of device d (slots d * 64 to (d + 1) * 64 - 1) name only that device's own column blocks d * 16 to (d + 1) * 16 - 1. `tile_rows`: the tile slots of device d = g * 32 + t name only row blocks of time blocks t - 1, t and t + 1 (rows k * 32 to (k + 1) * 32 - 1 belong to time block k). Only the first tile_count[d] slots of device d are live; some device has all 64 slots live.
All inputs are finite; a program needn't handle non-finite values.
Results may differ from the reference program's by a relative error of at most 0.0001.
Values sent between devices are 32-bit elements; how exact they have to be, the bound alone decides.
A program may use at most 64 MiB of HBM per device.

```python
import jax
import jax.numpy as jnp
from jax import lax

TILE = 128
CB_DEV = 16
RB_DEV = 32
NT_DEV = 64
NCLASS = 8
ITERS = 2
GCB = 512
NCB = 4096
NRB = 1024
NTILES = 16384
N_GRP = 8


def draw_tile_cols(key, part):
    device_ids = jnp.arange(NTILES, dtype=jnp.int32) // NT_DEV
    offsets = jax.random.randint(key, (NTILES,), 0, CB_DEV, dtype=jnp.int32)
    return device_ids * CB_DEV + offsets


def draw_tile_rows(key, part):
    time_count = GCB // CB_DEV
    own_time = jnp.arange(NTILES, dtype=jnp.int32) // NT_DEV % time_count
    picks = jax.random.randint(key, (NTILES,), 0, 6, dtype=jnp.int32)
    step_by = jnp.where(picks == 0, -1, jnp.where(picks == 1, 1, 0)).astype(jnp.int32)
    block_time = own_time + step_by
    block_time = jnp.where(block_time < 0, 1, block_time)
    block_time = jnp.where(block_time >= time_count, time_count - 2, block_time)
    offsets = jax.random.randint(jax.random.fold_in(key, 3), (NTILES,), 0, RB_DEV, dtype=jnp.int32)
    return block_time * RB_DEV + offsets


def draw_tile_count(key, part):
    device_total = NTILES // NT_DEV
    shifts = jax.random.randint(key, (device_total,), 0, 7, dtype=jnp.int32)
    counts = jnp.maximum(jnp.right_shift(jnp.full((device_total,), NT_DEV, jnp.int32), shifts), 1)
    busiest = jax.random.randint(jax.random.fold_in(key, 7), (), 0, device_total, dtype=jnp.int32)
    return counts.at[busiest].set(NT_DEV)


def with_ends(values, stream_key, least, high):
    longest = values.shape.index(max(values.shape))
    spots = []
    for shift in (0, 1):
        where = [jax.random.randint(jax.random.fold_in(stream_key, axis), (), 0, length) for axis, length in enumerate(values.shape)]
        where[longest] = (where[longest] + shift) % values.shape[longest]
        spots.append(tuple(where))
    return values.at[spots[0]].set(least).at[spots[1]].set(high)


def steps_of(own_key, dims, split, smallest, top_value):
    level = 1.0
    for dim, parts in split:
        steps = jax.random.uniform(jax.random.fold_in(jax.random.fold_in(own_key, 6), dim), (parts,), jnp.float32, smallest / len(split), top_value / len(split))
        level = level * jnp.repeat(jnp.exp(steps), dims[dim] // parts).reshape((-1,) + (1,) * (len(dims) - 1 - dim))
    return level


def centred(own_key, dims, scale, bound, cuts=(), kind=jnp.bfloat16):
    result = jax.random.normal(own_key, dims, jnp.float32) * scale
    if len(cuts) > 0:
        result = steps_of(own_key, dims, cuts, -0.22, 0.18) * result
    return jnp.clip(result, min=-bound, max=bound).astype(kind)


def setup_inputs(seed: int = 0) -> dict:
    seeds = jax.random.split(jax.random.key(seed), 12)
    x_start = centred(seeds[0], (NCB, TILE), 0.5, 3.0, ((0, 256),), jnp.float32)
    y_start = jnp.clip(1.0 * jax.random.uniform(seeds[1], (NRB, TILE), jnp.float32) ** steps_of(seeds[1], (NRB, TILE), ((0, 32),), -0.2, 0.2), 0.0, 1.0)
    cost = centred(seeds[2], (NCB, TILE), 1.0, 6.0, ((0, 256),), jnp.float32)
    rhs = centred(seeds[3], (NRB, TILE), 1.0, 6.0, ((0, 32),), jnp.float32)
    tiles = centred(seeds[4], (NTILES, TILE, TILE), (TILE * NT_DEV * N_GRP // (2 * RB_DEV)) ** -0.5, 0.1875, ((0, 256),), jnp.float32)
    tile_rows = draw_tile_rows(jax.random.fold_in(seeds[11], 71), 0)
    tile_cols = draw_tile_cols(jax.random.fold_in(seeds[11], 71), 0)
    tile_count = draw_tile_count(jax.random.fold_in(seeds[11], 71), 0)
    var_class = with_ends(jax.random.randint(seeds[8], (NCB, TILE), 0, NCLASS), jax.random.fold_in(seeds[8], 1), 0, NCLASS - 1).astype(jnp.int32)
    lower_table = jnp.clip(jax.random.uniform(seeds[9], (NCLASS,), jnp.float32, -1.0, -0.2), -1.0, -0.2)
    upper_table = jnp.clip(jax.random.uniform(seeds[10], (NCLASS,), jnp.float32, 0.2, 1.0), 0.2, 1.0)
    return {"x_start": x_start, "y_start": y_start, "cost": cost, "rhs": rhs, "tiles": tiles, "tile_rows": tile_rows, "tile_cols": tile_cols, "tile_count": tile_count, "var_class": var_class, "lower_table": lower_table, "upper_table": upper_table}


primal_step = 0.6
dual_step = 0.6


def reference(x_start, y_start, cost, rhs, tiles, tile_rows, tile_cols, tile_count, var_class, lower_table, upper_table):
    slot_ids = jnp.arange(NT_DEV, dtype=jnp.int32)
    live_mask = (slot_ids[None, :] < tile_count[:, None]).reshape(-1).astype(tiles.dtype)[:, None]
    lower_bound = lower_table[var_class]
    upper_bound = upper_table[var_class]

    def forward(field):
        picked = field[tile_cols]
        product = jnp.einsum("nrc,nc->nr", tiles, picked, precision=lax.Precision.HIGHEST) * live_mask
        return jnp.zeros((NRB, TILE), field.dtype).at[tile_rows].add(product)

    def adjoint(field):
        picked = field[tile_rows]
        product = jnp.einsum("nrc,nr->nc", tiles, picked, precision=lax.Precision.HIGHEST) * live_mask
        return jnp.zeros((NCB, TILE), field.dtype).at[tile_cols].add(product)

    primal = x_start
    dual = y_start
    primal_total = jnp.zeros_like(x_start)
    dual_total = jnp.zeros_like(y_start)
    for iteration in range(ITERS):
        moved = primal - primal_step * (cost - adjoint(dual))
        primal_next = jnp.minimum(jnp.maximum(moved, lower_bound), upper_bound)
        extrapolated = 2.0 * primal_next - primal
        dual_next = jnp.maximum(dual + dual_step * (rhs - forward(extrapolated)), 0.0)
        primal_total = primal_total + primal_next
        dual_total = dual_total + dual_next
        primal = primal_next
        dual = dual_next
    return (primal, dual, primal_total / ITERS, dual_total / ITERS)
```

```python
import jax
import jax.numpy as jnp
from jax import lax
from jax.experimental import pallas as pl
from jax.experimental.pallas import tpu as pltpu
from jax.sharding import PartitionSpec as P

ITERS = 2
STEP = 0.6
MESH = pl.DeviceIdType.MESH
F32 = jnp.float32
BF16 = jnp.bfloat16

NT = 64
TILE = 128
CB = 16
RB = 32
OWN = 4
PIECE = RB // OWN
WIN = 3 * RB
CHUNK = 8

SLOTS = {0: (0, 24, 0), 1: (24, 16, 0), -1: (40, 16, 1), 2: (56, 8, 0), -2: (64, 8, 2)}
SLOT_ROWS = 72


def split(value):
    high = value.astype(BF16)
    return high, (value - high.astype(F32)).astype(BF16)


def kernel(
    x_ref,
    y_ref,
    cost_ref,
    rhs_ref,
    tiles_ref,
    rows_ref,
    cols_ref,
    count_ref,
    rowv_ref,
    class_ref,
    lower_ref,
    upper_ref,
    primal_out,
    dual_out,
    staged,
    weights,
    placed,
    product,
    picked,
    window_y,
    window_rhs,
    window_next,
    terms_a,
    terms_b,
    parts_a,
    parts_b,
    piece_a,
    piece_b,
    last_dual,
    load_sem,
    dual_sems,
    send_sems,
    recv_sems,
):
    group = lax.axis_index("grp")
    time = lax.axis_index("tm")
    place = group // 2
    core = lax.rem(group, 2)
    is_owner = core == 1

    def at(distance):
        return lax.rem(time + distance + 32, 32)

    def owner(offset):
        return lax.rem(place + offset, OWN)

    def far(distance):
        here, there = time // 16, at(distance) // 16
        return here != there

    loads = []
    for chunk in range(NT // CHUNK):
        span = pl.ds(chunk * CHUNK, CHUNK)
        load = pltpu.make_async_copy(tiles_ref.at[span], staged.at[span], load_sem.at[chunk])
        load.start()
        loads.append(load)

    barrier = pltpu.get_barrier_semaphore()

    def greet(target_group, target_time):
        pl.semaphore_signal(
            barrier, inc=1, device_id=(target_group, target_time), device_id_type=MESH
        )

    @pl.when(is_owner)
    def _():
        for distance in (2, -2, 1, -1, 0):
            for offset in (3, 2, 1, 0):
                if distance or offset:
                    greet(2 * owner(offset) + 1, at(distance))
                greet(2 * owner(offset), at(distance))
        at_end = (place == 0) | (place == 3)
        more = [jnp.where(far(distance), jnp.where(at_end, 2, 0), 1) for distance in (1, -1)]
        pl.semaphore_wait(barrier, 5 * OWN - 1 + OWN + more[0] + more[1])

    @pl.when(jnp.logical_not(is_owner))
    def _():
        for distance in (1, -1):
            source = jnp.where(far(distance), jnp.where(place >= 2, 0, 3), place)
            greet(2 * source + 1, at(distance))
        for offset in range(OWN):
            greet(2 * owner(offset) + 1, time)
        pl.semaphore_wait(barrier, 5 * OWN)

    def dual_copies(distance):
        slot = 1 - distance
        crossing = far(distance)
        at_end = (place == 0) | (place == 3)
        first = jnp.where(crossing, jnp.where(place == 3, 0, 2), place)
        second = lax.rem(first + 1, 4)

        def copy(target, number):
            return pltpu.make_async_remote_copy(
                src_ref=y_ref,
                dst_ref=window_y.at[:, slot],
                send_sem=dual_sems.at[slot // 2 * 4 + number],
                recv_sem=recv_sems.at[0],
                device_id=(target, at(distance)),
                device_id_type=MESH,
            )

        pairs = [
            (is_owner & (jnp.logical_not(crossing) | at_end), [copy(2 * first, 0), copy(2 * first + 1, 1)]),
            (is_owner & crossing & at_end, [copy(2 * second, 2), copy(2 * second + 1, 3)]),
        ]
        return pairs

    def rhs_copy(distance):
        slot = 1 - distance
        return pltpu.make_async_remote_copy(
            src_ref=rhs_ref.at[place],
            dst_ref=window_rhs.at[slot],
            send_sem=send_sems.at[1],
            recv_sem=recv_sems.at[1],
            device_id=(group, at(distance)),
            device_id_type=MESH,
        )

    for distance in (1, -1):
        for when, copies in dual_copies(distance):

            @pl.when(when)
            def _():
                for copy in copies:
                    copy.start()

    @pl.when(is_owner)
    def _():
        for distance in (1, -1):
            rhs_copy(distance).start()

    window_y[:, 1] = y_ref[...]
    window_rhs[1] = rhs_ref[place]

    for chunk in range(NT // CHUNK):
        loads[chunk].wait()

        def halve(slot, carry):
            high, low = split(staged[slot])
            base = pl.multiple_of(slot * TILE, TILE)
            weights[pl.ds(base, TILE), 0:TILE] = high
            weights[pl.ds(base, TILE), TILE : 2 * TILE] = low
            return carry

        lax.fori_loop(chunk * CHUNK, (chunk + 1) * CHUNK, halve, 0)

    var_class = class_ref[...]
    lower = jnp.zeros((CB, TILE), F32)
    upper = jnp.zeros((CB, TILE), F32)
    for class_id in range(lower_ref.shape[0]):
        lower = jnp.where(var_class == class_id, lower_ref[class_id], lower)
        upper = jnp.where(var_class == class_id, upper_ref[class_id], upper)

    count = count_ref[0]
    first_row = (time - 1) * RB
    first_col = (group * 32 + time) * CB
    window_id = lax.broadcasted_iota(jnp.int32, (WIN, NT), 0)
    owner_id = window_id // (3 * PIECE)
    block_id = window_id // PIECE - 3 * owner_id
    row_id = block_id * RB + owner_id * PIECE + lax.rem(window_id, PIECE)
    slot_id = lax.broadcasted_iota(jnp.int32, (WIN, NT), 1)
    scatter = ((rowv_ref[...] - first_row) == row_id) & (slot_id < count)
    scatter = jnp.where(scatter, 1.0, 0.0)
    scatter = jnp.concatenate([scatter, scatter], axis=1).astype(BF16)

    sub_id = lax.broadcasted_iota(jnp.int32, (CB, TILE), 0)

    def adjoint(field):
        for slot in range(NT):
            row = jnp.clip(rows_ref[slot] - first_row, 0, WIN - 1)
            block = row // RB
            inner = row - block * RB
            part = inner // PIECE
            value = field[part, block, pl.ds(inner - part * PIECE, 1), :]
            col = jnp.where(slot < count, cols_ref[slot] - first_col, -1)
            here = sub_id == col
            high = value.astype(BF16).astype(F32)
            low = value - high
            span = slice(slot * TILE, (slot + 1) * TILE)
            placed[0:CB, span] = jnp.where(here, high, 0.0).astype(BF16)
            placed[CB : 2 * CB, span] = jnp.where(here, low, 0.0).astype(BF16)
        total = jnp.dot(placed[...], weights[...], preferred_element_type=F32)
        total = total[:CB] + total[CB:]
        return total[:, :TILE] + total[:, TILE:]

    def forward(field):
        high, low = split(field)
        both = jnp.concatenate([high, low], axis=0)
        both = jnp.concatenate([both, both], axis=1)
        result = lax.dot_general(
            both, weights[...], (((1,), (1,)), ((), ())), preferred_element_type=F32
        )
        for slot in range(NT):
            span = slice(slot * TILE, (slot + 1) * TILE)
            product[slot] = result[:CB, span] + result[CB:, span]
        for slot in range(NT):
            col = jnp.clip(cols_ref[slot] - first_col, 0, CB - 1)
            picked[slot : slot + 1, :] = product[slot, pl.ds(col, 1), :]
        high, low = split(picked[...])
        return jnp.dot(scatter, jnp.concatenate([high, low], axis=0), preferred_element_type=F32)

    def primal_update(primal, adjoint_part):
        moved = primal - STEP * (cost_ref[...] - adjoint_part)
        return jnp.minimum(jnp.maximum(moved, lower), upper)

    def to_owner(source, target, distance, offset, sems):
        return pltpu.make_async_remote_copy(
            src_ref=source,
            dst_ref=target,
            send_sem=send_sems.at[sems],
            recv_sem=recv_sems.at[sems],
            device_id=(2 * owner(offset) + 1, at(distance)),
            device_id_type=MESH,
        )

    def from_owner(source, target, offset, sems):
        return pltpu.make_async_remote_copy(
            src_ref=source,
            dst_ref=target,
            send_sem=send_sems.at[sems],
            recv_sem=recv_sems.at[sems],
            device_id=(lax.rem(group + offset, 8), time),
            device_id_type=MESH,
        )

    def spans_a(distance, offset):
        first, rows, block = SLOTS[-distance]
        source = terms_a.at[pl.ds(pl.multiple_of(owner(offset) * 3 * PIECE + block * PIECE, 8), rows)]
        return source, parts_a.at[pl.ds(pl.multiple_of(group * SLOT_ROWS + first, 8), rows)]

    def spans_b(distance, offset):
        source = terms_b.at[pl.ds(pl.multiple_of(owner(offset) * 3 * PIECE + (1 + distance) * PIECE, 8), PIECE)]
        return source, parts_b.at[pl.ds(pl.multiple_of(group * 3 * PIECE + (1 - distance) * PIECE, 8), PIECE)]

    def scatter_sum(distances, spans, sems):
        for distance in distances:
            for offset in (3, 2, 1, 0):
                source, target = spans(distance, offset)
                if distance or offset:
                    to_owner(source, target, distance, offset, sems).start()
                else:

                    @pl.when(jnp.logical_not(is_owner))
                    def _():
                        to_owner(source, target, distance, offset, sems).start()

    def wait_recv(ref, sems):
        pltpu.make_async_copy(ref, ref, recv_sems.at[sems]).wait()

    def wait_send(ref, sems):
        pltpu.make_async_copy(ref, ref, send_sems.at[sems]).wait()

    wait_recv(window_y.at[:, 0:2], 0)
    primal_0 = x_ref[...]
    primal_1 = primal_update(primal_0, adjoint(window_y))
    terms_a[...] = forward(2.0 * primal_1 - primal_0)
    scatter_sum((2, -2, 1, -1, 0), spans_a, 2)

    @pl.when(is_owner)
    def _():
        own = pl.ds(pl.multiple_of(place * 3 * PIECE, 8), 3 * PIECE)
        parts_a[pl.ds(pl.multiple_of(group * SLOT_ROWS, 8), 3 * PIECE)] = terms_a[own]
        wait_recv(window_rhs.at[0:2], 1)
        wait_recv(parts_a.at[0 : 8 * SLOT_ROWS - 3 * PIECE], 2)
        sums = jnp.sum(parts_a[...].reshape(8, SLOT_ROWS, TILE), axis=0)
        image = jnp.concatenate(
            [
                sums[0:8] + sums[40:48] + sums[64:72],
                sums[8:16] + sums[24:32] + sums[48:56],
                sums[16:24] + sums[32:40] + sums[56:64],
            ],
            axis=0,
        )
        for block in range(3):
            span = slice(block * PIECE, (block + 1) * PIECE)
            piece_a[block] = jnp.maximum(
                window_y[place, block] + STEP * (window_rhs[block] - image[span]), 0.0
            )
        for offset in range(7, 0, -1):
            from_owner(piece_a, window_next.at[place], offset, 3).start()
        window_next[place] = piece_a[...]
        wait_recv(window_next.at[0:3], 3)

    @pl.when(jnp.logical_not(is_owner))
    def _():
        wait_recv(window_next, 3)

    primal_2 = primal_update(primal_1, adjoint(window_next))
    terms_b[...] = forward(2.0 * primal_2 - primal_1)
    scatter_sum((1, -1, 0), spans_b, 4)
    primal_out[0] = primal_1
    primal_out[1] = primal_2
    dual_out[0] = window_next[:, 1]

    @pl.when(is_owner)
    def _():
        own = pl.ds(pl.multiple_of(place * 3 * PIECE + PIECE, 8), PIECE)
        parts_b[pl.ds(pl.multiple_of(group * 3 * PIECE + PIECE, 8), PIECE)] = terms_b[own]
        wait_recv(parts_b.at[0 : 23 * PIECE], 4)
        sums = jnp.sum(parts_b[...].reshape(8, 3 * PIECE, TILE), axis=0)
        image = sums[0:8] + sums[8:16] + sums[16:24]
        piece_b[...] = jnp.maximum(piece_a[1] + STEP * (window_rhs[1] - image), 0.0)
        for offset in range(7, 0, -1):
            from_owner(piece_b, last_dual.at[place], offset, 5).start()
        last_dual[place] = piece_b[...]
        wait_recv(last_dual.at[0:3], 5)

    @pl.when(jnp.logical_not(is_owner))
    def _():
        wait_recv(last_dual, 5)

    dual_out[1] = last_dual[...]

    for distance in (1, -1):
        for when, copies in dual_copies(distance):

            @pl.when(when)
            def _():
                for copy in copies:
                    copy.wait_send()

    @pl.when(is_owner)
    def _():
        wait_send(window_rhs.at[0:2], 1)
        wait_send(parts_a.at[0 : 33 * PIECE], 2)
        wait_send(parts_a.at[0 : 21 * PIECE], 3)
        wait_send(parts_a.at[0 : 11 * PIECE], 4)
        wait_send(parts_a.at[0 : 7 * PIECE], 5)

    @pl.when(jnp.logical_not(is_owner))
    def _():
        wait_send(parts_a.at[0 : 36 * PIECE], 2)
        wait_send(parts_a.at[0 : 12 * PIECE], 4)


def means(primals_ref, duals_ref, primal_out, dual_out, primal_mean_out, dual_mean_out):
    for iterates, last, mean in ((primals_ref, primal_out, primal_mean_out), (duals_ref, dual_out, dual_mean_out)):
        last[...] = iterates[1]
        mean[...] = (iterates[0] + iterates[1]) / ITERS


def body(
    x_start,
    y_start,
    cost,
    rhs,
    tiles,
    tile_rows,
    tile_cols,
    tile_count,
    var_class,
    lower_table,
    upper_table,
):
    vmem = pl.BlockSpec(memory_space=pltpu.VMEM)
    smem = pl.BlockSpec(memory_space=pltpu.SMEM)
    primals, duals = pl.pallas_call(
        kernel,
        name="pdhg",
        out_shape=(
            jax.ShapeDtypeStruct((ITERS, CB, TILE), F32),
            jax.ShapeDtypeStruct((ITERS, OWN, PIECE, TILE), F32),
        ),
        in_specs=[vmem, vmem, vmem, vmem, pl.BlockSpec(memory_space=pl.ANY), smem, smem, smem, vmem, vmem, smem, smem],
        out_specs=(vmem, vmem),
        scratch_shapes=[
            pltpu.VMEM((NT, TILE, TILE), F32),
            pltpu.VMEM((NT * TILE, 2 * TILE), BF16),
            pltpu.VMEM((2 * CB, NT * TILE), BF16),
            pltpu.VMEM((NT, CB, TILE), F32),
            pltpu.VMEM((NT, TILE), F32),
            pltpu.VMEM((OWN, 3, PIECE, TILE), F32),
            pltpu.VMEM((3, PIECE, TILE), F32),
            pltpu.VMEM((OWN, 3, PIECE, TILE), F32),
            pltpu.VMEM((WIN, TILE), F32),
            pltpu.VMEM((WIN, TILE), F32),
            pltpu.VMEM((8 * SLOT_ROWS, TILE), F32),
            pltpu.VMEM((8 * 3 * PIECE, TILE), F32),
            pltpu.VMEM((3, PIECE, TILE), F32),
            pltpu.VMEM((PIECE, TILE), F32),
            pltpu.VMEM((OWN, PIECE, TILE), F32),
            pltpu.SemaphoreType.DMA((NT // CHUNK,)),
            pltpu.SemaphoreType.DMA((8,)),
            pltpu.SemaphoreType.DMA((6,)),
            pltpu.SemaphoreType.DMA((6,)),
        ],
        compiler_params=pltpu.CompilerParams(
            collective_id=0, has_side_effects=True, vmem_limit_bytes=60 * 1024 * 1024
        ),
    )(
        x_start,
        y_start.reshape(OWN, PIECE, TILE),
        cost,
        rhs.reshape(OWN, PIECE, TILE),
        tiles,
        tile_rows,
        tile_cols,
        tile_count,
        tile_rows.reshape(1, NT),
        var_class,
        lower_table,
        upper_table,
    )
    columns = jax.ShapeDtypeStruct((CB, TILE), F32)
    rows = jax.ShapeDtypeStruct((RB, TILE), F32)
    return pl.pallas_call(
        means,
        name="means",
        out_shape=(columns, rows, columns, rows),
        in_specs=[vmem, vmem],
        out_specs=(vmem, vmem, vmem, vmem),
    )(primals, duals.reshape(ITERS, RB, TILE))


def solution(mesh):
    return jax.shard_map(
        body,
        mesh=mesh,
        in_specs=(
            P(("grp", "tm"), None),
            P("tm", None),
            P(("grp", "tm"), None),
            P("tm", None),
            P(("grp", "tm"), None, None),
            P(("grp", "tm")),
            P(("grp", "tm")),
            P(("grp", "tm")),
            P(("grp", "tm"), None),
            P(),
            P(),
        ),
        out_specs=(P(("grp", "tm"), None), P("tm", None), P(("grp", "tm"), None), P("tm", None)),
        check_vma=False,
    )
```

```python
import jax
import jax.numpy as jnp
from jax import lax
from jax.experimental import pallas as pl
from jax.experimental.pallas import tpu as pltpu
from jax.sharding import PartitionSpec as P

ITERS = 2
STEP = 0.6
MESH = pl.DeviceIdType.MESH
F32 = jnp.float32
BF16 = jnp.bfloat16

NT = 64
TILE = 128
CB = 16
RB = 32
OWN = 4
PIECE = RB // OWN
WIN = 3 * RB
CHUNK = 8

LAST, NEXT = 15, 16
SLOT_ROWS = 6 * PIECE


def split(value):
    high = value.astype(BF16)
    return high, (value - high.astype(F32)).astype(BF16)


def kernel(
    x_hbm,
    y_hbm,
    cost_hbm,
    rhs_hbm,
    tiles_hbm,
    cols_hbm,
    count_hbm,
    rowv_hbm,
    colv_hbm,
    class_hbm,
    lower_hbm,
    upper_hbm,
    primal_out,
    dual_out,
    x_ref,
    y_ref,
    cost_ref,
    rhs_ref,
    cols_ref,
    count_ref,
    rowv_ref,
    colv_ref,
    class_ref,
    lower_ref,
    upper_ref,
    staged,
    turned,
    factors,
    select,
    partial,
    pick,
    window_y,
    window_rhs,
    window_next,
    terms_a,
    terms_b,
    parts_a,
    parts_b,
    piece_a,
    piece_b,
    last_dual,
    load_sem,
    input_sems,
    dual_sems,
    halo_sems,
    sums_sent,
    sums_recv,
    send_sems,
    recv_sems,
):
    group = lax.axis_index("grp")
    time = lax.axis_index("tm")
    place = group // 2
    core = lax.rem(group, 2)
    is_owner = core == 1

    def at(distance):
        return time + distance

    def exists(distance):
        there = time + distance
        return (there >= 0) & (there < 32)

    def number(distances):
        return sum(jnp.where(exists(distance), 1, 0) for distance in distances)

    def owner(offset):
        return lax.rem(place + offset, OWN)

    def far(distance):
        return (time == LAST) if distance > 0 else (time == NEXT)

    def near(distance):
        return exists(distance) & jnp.logical_not(far(distance))

    edge = (time == LAST) | (time == NEXT)
    at_end = (place == 0) | (place == 3)

    def both(distance):
        return edge if distance == 0 else far(distance)

    parts_a[...] = jnp.zeros_like(parts_a)
    parts_b[...] = jnp.zeros_like(parts_b)
    window_y[...] = jnp.zeros_like(window_y)
    window_next[...] = jnp.zeros_like(window_next)
    window_rhs[...] = jnp.zeros_like(window_rhs)

    barrier = pltpu.get_barrier_semaphore()

    def greet(target_group, target_time):
        pl.semaphore_signal(
            barrier, inc=1, device_id=(target_group, target_time), device_id_type=MESH
        )

    def greet_all(distance):
        for offset in (3, 2, 1, 0):
            if distance or offset:
                greet(2 * owner(offset) + 1, at(distance))
            greet(2 * owner(offset), at(distance))

    @pl.when(is_owner)
    def _():
        for distance, when in ((2, time == LAST), (-2, time == NEXT), (1, exists(1)), (-1, exists(-1))):

            @pl.when(when)
            def _():
                greet_all(distance)

        greet_all(0)

    @pl.when(jnp.logical_not(is_owner))
    def _():
        for distance in (1, -1):

            @pl.when(far(distance))
            def _():
                greet(2 * jnp.where(place >= 2, 0, 3) + 1, at(distance))

            @pl.when(near(distance))
            def _():
                for offset in range(OWN):
                    greet(2 * owner(offset) + 1, at(distance))

        for offset in range(OWN):
            greet(2 * owner(offset) + 1, time)

    inputs = []
    for index, (source, target) in enumerate(
        (
            (y_hbm, y_ref),
            (rhs_hbm, rhs_ref),
            (x_hbm, x_ref),
            (cost_hbm, cost_ref),
            (class_hbm, class_ref),
            (rowv_hbm, rowv_ref),
            (colv_hbm, colv_ref),
            (count_hbm, count_ref),
            (lower_hbm, lower_ref),
            (upper_hbm, upper_ref),
            (cols_hbm, cols_ref),
        )
    ):
        copy = pltpu.make_async_copy(source, target, input_sems.at[index])
        copy.start()
        inputs.append(copy)
    loads = []
    for chunk in range(NT // CHUNK):
        span = pl.ds(chunk * CHUNK, CHUNK)
        load = pltpu.make_async_copy(tiles_hbm.at[span], staged.at[span], load_sem.at[chunk])
        load.start()
        loads.append(load)
    for copy in inputs:
        copy.wait()

    of_owner = 7
    for distance in (1, -1):
        of_owner = of_owner + jnp.where(near(distance), 8, 0)
        of_owner = of_owner + jnp.where(far(distance), jnp.where(at_end, 6, 4), 0)
    two_steps = jnp.where((time == LAST - 1) | (time == NEXT + 1), OWN, 0)
    of_other = OWN * number((1, 0, -1))
    pl.semaphore_wait(barrier, jnp.where(is_owner, of_owner, of_other) + two_steps)

    def dual_copies(distance):
        slot = 1 - distance
        crossing = far(distance)
        first = jnp.where(crossing, jnp.where(place == 3, 0, 2), place)
        second = lax.rem(first + 1, 4)

        def copy(target, number):
            return pltpu.make_async_remote_copy(
                src_ref=y_ref,
                dst_ref=window_y.at[:, slot],
                send_sem=dual_sems.at[slot // 2 * 4 + number],
                recv_sem=halo_sems.at[slot],
                device_id=(target, at(distance)),
                device_id_type=MESH,
            )

        pairs = [
            (is_owner & exists(distance) & (jnp.logical_not(crossing) | at_end), [copy(2 * first, 0), copy(2 * first + 1, 1)]),
            (is_owner & crossing & at_end, [copy(2 * second, 2), copy(2 * second + 1, 3)]),
        ]
        return pairs

    def rhs_copy(distance):
        slot = 1 - distance
        return pltpu.make_async_remote_copy(
            src_ref=rhs_ref.at[place],
            dst_ref=window_rhs.at[slot],
            send_sem=halo_sems.at[slot + 4],
            recv_sem=halo_sems.at[slot + 1],
            device_id=(group, at(distance)),
            device_id_type=MESH,
        )

    for distance in (1, -1):
        for when, copies in dual_copies(distance):

            @pl.when(when)
            def _():
                for copy in copies:
                    copy.start()

    @pl.when(is_owner)
    def _():
        for distance in (1, -1):

            @pl.when(far(distance))
            def _():
                rhs_copy(distance).start()

    window_y[:, 1] = y_ref[...]
    window_rhs[1] = rhs_ref[place]

    for chunk in range(NT // CHUNK):
        loads[chunk].wait()

        def turn(slot, carry):
            turned[slot] = staged[slot].T
            return carry

        lax.fori_loop(chunk * CHUNK, (chunk + 1) * CHUNK, turn, 0, unroll=4)

    var_class = class_ref[...]
    lower = jnp.zeros((CB, TILE), F32)
    upper = jnp.zeros((CB, TILE), F32)
    for class_id in range(lower_ref.shape[1]):
        lower = jnp.where(var_class == class_id, lower_ref[:, class_id : class_id + 1], lower)
        upper = jnp.where(var_class == class_id, upper_ref[:, class_id : class_id + 1], upper)

    first_row = (time - 1) * RB
    first_col = (group * 32 + time) * CB
    slot_id = lax.broadcasted_iota(jnp.int32, (WIN, NT), 1)
    window_id = lax.broadcasted_iota(jnp.int32, (WIN, NT), 0)
    owner_id = window_id // (3 * PIECE)
    block_id = window_id // PIECE - 3 * owner_id
    row_id = block_id * RB + owner_id * PIECE + lax.rem(window_id, PIECE)
    scatter = ((rowv_ref[...] - first_row) == row_id) & (slot_id < count_ref[0])
    gather = ((colv_ref[...] - first_col) == window_id[:CB]) & (slot_id[:CB] < count_ref[0])
    scatter = jnp.where(scatter, 1.0, 0.0)
    chosen = jnp.concatenate([scatter, jnp.where(gather, 1.0, 0.0)], axis=0)
    pick[...] = jnp.concatenate([scatter, scatter], axis=0).astype(BF16)
    spread = lax.broadcasted_iota(jnp.int32, (NT, 8 * NT), 1) // 8 == lax.broadcasted_iota(jnp.int32, (NT, 8 * NT), 0)
    chosen = jnp.dot(chosen.astype(BF16), jnp.where(spread, 1.0, 0.0).astype(BF16), preferred_element_type=F32)
    chosen = chosen.astype(BF16)
    select[...] = jnp.concatenate([chosen, chosen], axis=1)

    def add_up(first, last):
        high, low = split(partial[...])
        return jnp.dot(
            select[first:last], jnp.concatenate([high, low], axis=0), preferred_element_type=F32
        )

    def fold(value):
        return jnp.sum(value.reshape(TILE // 8, 8, TILE), axis=0)

    def adjoint(field):
        high, low = split(field[...].reshape(WIN, TILE).T)
        columns = jnp.dot(
            jnp.concatenate([high, low], axis=1), pick[...], preferred_element_type=F32
        )
        for slot in range(NT):
            factor = jnp.broadcast_to(columns[:, slot : slot + 1], (TILE, TILE))
            partial[8 * slot : 8 * slot + 8] = fold(staged[slot] * factor)
        return add_up(WIN, WIN + CB)

    def forward(field):
        columns = field.T
        for block in range(CB):
            factors[block] = jnp.broadcast_to(columns[:, block : block + 1], (TILE, TILE))
        for slot in range(NT):
            col = jnp.clip(cols_ref[slot] - first_col, 0, CB - 1)
            partial[8 * slot : 8 * slot + 8] = fold(turned[slot] * factors[col])
        return add_up(0, WIN)

    def primal_update(primal, adjoint_part):
        moved = primal - STEP * (cost_ref[...] - adjoint_part)
        return jnp.minimum(jnp.maximum(moved, lower), upper)

    def to_owner(source, target, distance, offset, sems):
        return pltpu.make_async_remote_copy(
            src_ref=source,
            dst_ref=target,
            send_sem=sums_sent.at[sems, distance + 2],
            recv_sem=sums_recv.at[sems, 2 - distance],
            device_id=(2 * owner(offset) + 1, at(distance)),
            device_id_type=MESH,
        )

    def from_owner(source, target, offset, distance, semaphore):
        return pltpu.make_async_remote_copy(
            src_ref=source,
            dst_ref=target,
            send_sem=send_sems.at[semaphore],
            recv_sem=recv_sems.at[semaphore],
            device_id=(lax.rem(group + offset, 8), at(distance)),
            device_id_type=MESH,
        )

    def rows_of(ref, first, pieces):
        return ref.at[pl.ds(pl.multiple_of(first, PIECE), pieces * PIECE)]

    def copy_a(distance, offset, pieces):
        block = jnp.where(time == NEXT, 0, 1) if distance == 0 else 2 if distance > 0 else 0
        if pieces == 2:
            block = jnp.where(time == NEXT, 0, 1)
        region = {
            0: 0,
            1: jnp.where(time + 1 == NEXT, 2, 4),
            -1: jnp.where(time - 1 == NEXT, 4, 2),
            2: 5,
            -2: 5,
        }[distance]
        if distance == 0 and pieces == 1:
            block = 1
        source = rows_of(terms_a, (owner(offset) * 3 + block) * PIECE, pieces)
        target = rows_of(parts_a, group * SLOT_ROWS + region * PIECE, pieces)
        return to_owner(source, target, distance, offset, 0)

    def copy_b(distance, offset):
        source = rows_of(terms_b, (owner(offset) * 3 + 1 + distance) * PIECE, 1)
        target = rows_of(parts_b, (group * 3 + 1 - distance) * PIECE, 1)
        return to_owner(source, target, distance, offset, 1)

    def to_owners(distance, copy):
        for offset in (3, 2, 1, 0):
            if distance or offset:
                copy(distance, offset).start()
            else:

                @pl.when(jnp.logical_not(is_owner))
                def _():
                    copy(distance, offset).start()

    def steps_a():
        for distance in (1, -1, 0):
            yield distance, exists(distance) & both(distance), 2
        for distance in (1, -1, 0):
            yield distance, exists(distance) & jnp.logical_not(both(distance)), 1

    def wait_rows(semaphore, pieces):
        ref = parts_a.at[0 : pieces * PIECE]
        pltpu.make_async_copy(ref, ref, semaphore).wait()

    def wait_sums_a(semaphores, two_steps, copies, own):
        for distance, when, pieces in steps_a():

            @pl.when(when)
            def _():
                wait_rows(semaphores.at[0, distance + 2], pieces * (copies if distance else own))

        for distance, when in two_steps:

            @pl.when(when)
            def _():
                wait_rows(semaphores.at[0, distance + 2], copies)

    def wait_sums_b(semaphores, copies, own):
        for distance in (1, -1, 0):

            @pl.when(exists(distance))
            def _():
                wait_rows(semaphores.at[1, distance + 2], copies if distance else own)

    for distance in (1, -1):

        @pl.when(exists(distance))
        def _():
            dual_in = window_y.at[:, 1 + distance]
            pltpu.make_async_copy(dual_in, dual_in, halo_sems.at[1 + distance]).wait()

    primal_0 = x_ref[...]
    primal_1 = primal_update(primal_0, adjoint(window_y))
    terms_a[...] = forward(2.0 * primal_1 - primal_0)
    for distance, when in ((2, time == LAST - 1), (-2, time == NEXT + 1)):

        @pl.when(when)
        def _():
            to_owners(distance, lambda distance, offset: copy_a(distance, offset, 1))

    for distance, when, pieces in steps_a():

        @pl.when(when)
        def _():
            to_owners(distance, lambda distance, offset: copy_a(distance, offset, pieces))

    @pl.when(is_owner)
    def _():
        for pieces, when in ((2, edge), (1, jnp.logical_not(edge))):

            @pl.when(when)
            def _():
                block = jnp.where(time == NEXT, 0, 1) if pieces == 2 else 1
                source = pl.ds(pl.multiple_of((place * 3 + block) * PIECE, 8), pieces * PIECE)
                target = pl.ds(pl.multiple_of(group * SLOT_ROWS, 8), pieces * PIECE)
                parts_a[target] = terms_a[source]

        for distance in (1, -1):

            @pl.when(far(distance))
            def _():
                rhs_in = window_rhs.at[1 + distance]
                pltpu.make_async_copy(rhs_in, rhs_in, halo_sems.at[2 + distance]).wait()

        wait_sums_a(sums_recv, ((2, time == LAST), (-2, time == NEXT)), 8, 7)
        sums = jnp.sum(parts_a[...].reshape(8, SLOT_ROWS, TILE), axis=0)
        low = sums[0:8] + sums[16:24]
        high = sums[8:16] + sums[24:32]
        upper_side = time == NEXT
        first = jnp.where(upper_side, high, low) + sums[32:40]
        second = jnp.where(upper_side, low, high) + sums[40:48]
        for block in range(3):
            image = first if block == 1 else second
            piece_a[block] = jnp.maximum(window_y[place, block] + STEP * (window_rhs[block] - image), 0.0)
        for distance in (1, -1):

            @pl.when(near(distance))
            def _():
                for offset in range(7, -1, -1):
                    from_owner(
                        piece_a.at[1], window_next.at[place, 1 - distance], offset, distance, 2 + distance
                    ).start()

        @pl.when(edge)
        def _():
            span = pl.ds(jnp.where(time == NEXT, 0, 1), 2)
            for offset in range(7, 0, -1):
                from_owner(piece_a.at[span], window_next.at[place, span], offset, 0, 0).start()
            window_next[place, span] = piece_a[span]

        @pl.when(jnp.logical_not(edge))
        def _():
            for offset in range(7, 0, -1):
                from_owner(piece_a.at[1], window_next.at[place, 1], offset, 0, 0).start()
            window_next[place, 1] = piece_a[1]

    for owned, others in ((is_owner, OWN - 1), (jnp.logical_not(is_owner), OWN)):
        for pieces, when in ((2, edge), (1, jnp.logical_not(edge))):

            @pl.when(owned & when)
            def _():
                wait_rows(recv_sems.at[0], pieces * others)

    for distance in (1, -1):

        @pl.when(near(distance))
        def _():
            wait_rows(recv_sems.at[2 - distance], OWN)

    primal_2 = primal_update(primal_1, adjoint(window_next))
    terms_b[...] = forward(2.0 * primal_2 - primal_1)
    for distance in (1, -1, 0):

        @pl.when(exists(distance))
        def _():
            to_owners(distance, copy_b)

    primal_out[0] = primal_1
    primal_out[1] = primal_2
    dual_out[0] = window_next[:, 1]

    @pl.when(is_owner)
    def _():
        own = pl.ds(pl.multiple_of(place * 3 * PIECE + PIECE, 8), PIECE)
        parts_b[pl.ds(pl.multiple_of(group * 3 * PIECE + PIECE, 8), PIECE)] = terms_b[own]
        wait_sums_b(sums_recv, 8, 7)
        sums = jnp.sum(parts_b[...].reshape(8, 3 * PIECE, TILE), axis=0)
        image = sums[0:8] + sums[8:16] + sums[16:24]
        piece_b[...] = jnp.maximum(piece_a[1] + STEP * (window_rhs[1] - image), 0.0)
        for offset in range(7, 0, -1):
            from_owner(piece_b, last_dual.at[place], offset, 0, 2).start()
        last_dual[place] = piece_b[...]
        wait_rows(recv_sems.at[2], OWN - 1)

    @pl.when(jnp.logical_not(is_owner))
    def _():
        wait_rows(recv_sems.at[2], OWN)

    dual_out[1] = last_dual[...]

    for distance in (1, -1):
        for when, copies in dual_copies(distance):

            @pl.when(when)
            def _():
                for copy in copies:
                    copy.wait_send()

    two_steps = ((2, time == LAST - 1), (-2, time == NEXT + 1))

    @pl.when(is_owner)
    def _():
        for distance in (1, -1):

            @pl.when(far(distance))
            def _():
                rhs_copy(distance).wait_send()

            @pl.when(near(distance))
            def _():
                wait_rows(send_sems.at[2 + distance], 8)

        wait_sums_a(sums_sent, two_steps, OWN, OWN - 1)
        wait_sums_b(sums_sent, OWN, OWN - 1)
        for pieces, when in ((2, edge), (1, jnp.logical_not(edge))):

            @pl.when(when)
            def _():
                wait_rows(send_sems.at[0], 7 * pieces)

        wait_rows(send_sems.at[2], 7)

    @pl.when(jnp.logical_not(is_owner))
    def _():
        wait_sums_a(sums_sent, two_steps, OWN, OWN)
        wait_sums_b(sums_sent, OWN, OWN)


def means(primals_ref, duals_ref, primal_out, dual_out, primal_mean_out, dual_mean_out):
    for iterates, last, mean in ((primals_ref, primal_out, primal_mean_out), (duals_ref, dual_out, dual_mean_out)):
        last[...] = iterates[1]
        mean[...] = (iterates[0] + iterates[1]) / ITERS


def body(
    x_start,
    y_start,
    cost,
    rhs,
    tiles,
    tile_rows,
    tile_cols,
    tile_count,
    var_class,
    lower_table,
    upper_table,
):
    vmem = pl.BlockSpec(memory_space=pltpu.VMEM)
    primals, duals = pl.pallas_call(
        kernel,
        name="pdhg",
        out_shape=(
            jax.ShapeDtypeStruct((ITERS, CB, TILE), F32),
            jax.ShapeDtypeStruct((ITERS, OWN, PIECE, TILE), F32),
        ),
        in_specs=[pl.BlockSpec(memory_space=pltpu.HBM)] * 12,
        out_specs=(vmem, vmem),
        scratch_shapes=[
            pltpu.VMEM((CB, TILE), F32),
            pltpu.VMEM((OWN, PIECE, TILE), F32),
            pltpu.VMEM((CB, TILE), F32),
            pltpu.VMEM((OWN, PIECE, TILE), F32),
            pltpu.SMEM((NT,), jnp.int32),
            pltpu.SMEM((1,), jnp.int32),
            pltpu.VMEM((1, NT), jnp.int32),
            pltpu.VMEM((1, NT), jnp.int32),
            pltpu.VMEM((CB, TILE), jnp.int32),
            pltpu.VMEM((1, 8), F32),
            pltpu.VMEM((1, 8), F32),
            pltpu.VMEM((NT, TILE, TILE), F32),
            pltpu.VMEM((NT, TILE, TILE), F32),
            pltpu.VMEM((CB, TILE, TILE), F32),
            pltpu.VMEM((WIN + CB, 16 * NT), BF16),
            pltpu.VMEM((8 * NT, TILE), F32),
            pltpu.VMEM((2 * WIN, NT), BF16),
            pltpu.VMEM((OWN, 3, PIECE, TILE), F32),
            pltpu.VMEM((3, PIECE, TILE), F32),
            pltpu.VMEM((OWN, 3, PIECE, TILE), F32),
            pltpu.VMEM((WIN, TILE), F32),
            pltpu.VMEM((WIN, TILE), F32),
            pltpu.VMEM((8 * SLOT_ROWS, TILE), F32),
            pltpu.VMEM((8 * 3 * PIECE, TILE), F32),
            pltpu.VMEM((3, PIECE, TILE), F32),
            pltpu.VMEM((PIECE, TILE), F32),
            pltpu.VMEM((OWN, PIECE, TILE), F32),
            pltpu.SemaphoreType.DMA((NT // CHUNK,)),
            pltpu.SemaphoreType.DMA((11,)),
            pltpu.SemaphoreType.DMA((8,)),
            pltpu.SemaphoreType.DMA((8,)),
            pltpu.SemaphoreType.DMA((2, 5)),
            pltpu.SemaphoreType.DMA((2, 5)),
            pltpu.SemaphoreType.DMA((4,)),
            pltpu.SemaphoreType.DMA((4,)),
        ],
        compiler_params=pltpu.CompilerParams(
            collective_id=0, has_side_effects=True, vmem_limit_bytes=60 * 1024 * 1024
        ),
    )(
        x_start,
        y_start.reshape(OWN, PIECE, TILE),
        cost,
        rhs.reshape(OWN, PIECE, TILE),
        tiles,
        tile_cols,
        tile_count,
        tile_rows.reshape(1, NT),
        tile_cols.reshape(1, NT),
        var_class,
        lower_table.reshape(1, 8),
        upper_table.reshape(1, 8),
    )
    columns = jax.ShapeDtypeStruct((CB, TILE), F32)
    rows = jax.ShapeDtypeStruct((RB, TILE), F32)
    return pl.pallas_call(
        means,
        name="means",
        out_shape=(columns, rows, columns, rows),
        in_specs=[vmem, vmem],
        out_specs=(vmem, vmem, vmem, vmem),
    )(primals, duals.reshape(ITERS, RB, TILE))


def solution(mesh):
    return jax.shard_map(
        body,
        mesh=mesh,
        in_specs=(
            P(("grp", "tm"), None),
            P("tm", None),
            P(("grp", "tm"), None),
            P("tm", None),
            P(("grp", "tm"), None, None),
            P(("grp", "tm")),
            P(("grp", "tm")),
            P(("grp", "tm")),
            P(("grp", "tm"), None),
            P(),
            P(),
        ),
        out_specs=(P(("grp", "tm"), None), P("tm", None), P(("grp", "tm"), None), P("tm", None)),
        check_vma=False,
    )
```

```python
import jax
import jax.numpy as jnp
from jax import lax
from jax.experimental import pallas as pl
from jax.experimental.pallas import tpu as pltpu
from jax.sharding import PartitionSpec as P

ITERS = 2
STEP = 0.6
MESH = pl.DeviceIdType.MESH
F32 = jnp.float32
BF16 = jnp.bfloat16

NT = 64
TILE = 128
CB = 16
RB = 32
OWN = 2
PIECE = RB // OWN
WIN = 3 * RB
CHUNK = 8
AM = 24
FM = 16
HALVED = max(AM, FM)

LAST, NEXT = 15, 16
SLOT_ROWS = 6 * PIECE


def split(value):
    high = value.astype(BF16)
    return high, (value - high.astype(F32)).astype(BF16)


def kernel(
    x_hbm,
    y_hbm,
    cost_hbm,
    rhs_hbm,
    tiles_hbm,
    cols_hbm,
    count_hbm,
    rowv_hbm,
    colv_hbm,
    class_hbm,
    lower_hbm,
    upper_hbm,
    primal_out,
    dual_out,
    x_ref,
    y_ref,
    cost_ref,
    rhs_ref,
    cols_ref,
    count_ref,
    rowv_ref,
    colv_ref,
    class_ref,
    lower_ref,
    upper_ref,
    staged,
    turned,
    factors,
    weights,
    placed,
    product,
    select_f,
    select_a,
    partial,
    pick,
    pick_last,
    window_y,
    window_rhs,
    window_next,
    terms_a,
    terms_b,
    parts_a,
    parts_b,
    piece_a,
    piece_b,
    last_dual,
    load_sem,
    input_sems,
    dual_sems,
    halo_sems,
    sums_sent,
    sums_recv,
    send_sems,
    recv_sems,
):
    group = lax.axis_index("grp")
    time = lax.axis_index("tm")
    place = group // 2
    core = lax.rem(group, 2)
    on_core = core == 1
    is_owner = on_core & ((place == 1) | (place == 2))
    mine = place // 2

    def at(distance):
        return time + distance

    def exists(distance):
        there = time + distance
        return (there >= 0) & (there < 32)

    def number(distances):
        return sum(jnp.where(exists(distance), 1, 0) for distance in distances)

    def owner(offset):
        return lax.rem(mine + offset, OWN)

    def owner_group(offset):
        return 2 * owner(offset) + 3

    def far(distance):
        return (time == LAST) if distance > 0 else (time == NEXT)

    def near(distance):
        return exists(distance) & jnp.logical_not(far(distance))

    edge = (time == LAST) | (time == NEXT)
    at_end = (place == 0) | (place == 3)

    def both(distance):
        return edge if distance == 0 else far(distance)

    parts_a[...] = jnp.zeros_like(parts_a)
    parts_b[...] = jnp.zeros_like(parts_b)
    window_y[...] = jnp.zeros_like(window_y)
    window_next[...] = jnp.zeros_like(window_next)
    window_rhs[...] = jnp.zeros_like(window_rhs)

    barrier = pltpu.get_barrier_semaphore()

    def greet(target_group, target_time):
        pl.semaphore_signal(
            barrier, inc=1, device_id=(target_group, target_time), device_id_type=MESH
        )

    def greet_all(distance):
        for offset in range(7, -1, -1):
            if distance or offset:
                greet(lax.rem(group + offset, 8), at(distance))

    source_place = jnp.where(place >= 2, 0, 3)
    left = jnp.where(place == 3, 0, 2)

    @pl.when(is_owner)
    def _():
        for distance, when in ((2, time == LAST), (-2, time == NEXT), (1, exists(1)), (-1, exists(-1))):

            @pl.when(when)
            def _():
                greet_all(distance)

        greet_all(0)

    @pl.when(jnp.logical_not(is_owner))
    def _():
        for distance in (1, -1):

            @pl.when(on_core & far(distance))
            def _():
                greet(2 * source_place + 1, at(distance))

            @pl.when(on_core & near(distance))
            def _():
                greet(group, at(distance))

            @pl.when(near(distance))
            def _():
                for offset in range(OWN):
                    greet(owner_group(offset), at(distance))

        for offset in range(OWN):
            greet(owner_group(offset), time)

        @pl.when(jnp.logical_not(on_core) & at_end)
        def _():
            greet(group + 1, time)

    inputs = []
    for index, (source, target) in enumerate(
        (
            (y_hbm, y_ref),
            (rhs_hbm, rhs_ref),
            (x_hbm, x_ref),
            (cost_hbm, cost_ref),
            (class_hbm, class_ref),
            (rowv_hbm, rowv_ref),
            (colv_hbm, colv_ref),
            (count_hbm, count_ref),
            (lower_hbm, lower_ref),
            (upper_hbm, upper_ref),
            (cols_hbm, cols_ref),
        )
    ):
        copy = pltpu.make_async_copy(source, target, input_sems.at[index])
        copy.start()
        inputs.append(copy)
    loads = []
    for chunk in range(NT // CHUNK):
        span = pl.ds(chunk * CHUNK, CHUNK)
        load = pltpu.make_async_copy(tiles_hbm.at[span], staged.at[span], load_sem.at[chunk])
        load.start()
        loads.append(load)
    for copy in inputs:
        copy.wait()

    of_owner = 7
    for distance in (1, -1):
        of_owner = of_owner + jnp.where(near(distance), 8, 0)
        of_owner = of_owner + jnp.where(far(distance), OWN, 0)
    two_steps = jnp.where((time == LAST - 1) | (time == NEXT + 1), OWN, 0)
    of_other = OWN * number((1, 0, -1))
    of_sender = of_other + number((1, -1)) + 1
    peers = jnp.where(is_owner, of_owner, jnp.where(on_core, of_sender, of_other))
    pl.semaphore_wait(barrier, peers + two_steps)

    def dual_copies(distance):
        slot = 1 - distance

        def copy(target, number):
            return pltpu.make_async_remote_copy(
                src_ref=y_ref,
                dst_ref=window_y.at[:, slot],
                send_sem=dual_sems.at[slot // 2 * 4 + number],
                recv_sem=halo_sems.at[slot],
                device_id=(2 * target + 1, at(distance)),
                device_id_type=MESH,
            )

        return [
            (on_core & far(distance) & at_end, [copy(left, 0), copy(left + 1, 1)]),
            (on_core & near(distance), [copy(place, 2)]),
        ]

    def pass_on(distance):
        slot = 1 + distance
        return pltpu.make_async_remote_copy(
            src_ref=window_y.at[:, slot],
            dst_ref=window_y.at[:, slot],
            send_sem=dual_sems.at[slot // 2 * 4 + 3],
            recv_sem=halo_sems.at[slot],
            device_id=(group - 1, time),
            device_id_type=MESH,
        )

    def rhs_copy(distance):
        slot = 1 - distance
        return pltpu.make_async_remote_copy(
            src_ref=rhs_ref.at[mine],
            dst_ref=window_rhs.at[slot],
            send_sem=halo_sems.at[slot + 4],
            recv_sem=halo_sems.at[slot + 1],
            device_id=(group, at(distance)),
            device_id_type=MESH,
        )

    for distance in (1, -1):
        for when, copies in dual_copies(distance):

            @pl.when(when)
            def _():
                for copy in copies:
                    copy.start()

    @pl.when(is_owner)
    def _():
        for distance in (1, -1):

            @pl.when(far(distance))
            def _():
                rhs_copy(distance).start()

    window_y[:, 1] = y_ref[...]
    window_rhs[1] = rhs_ref[mine]

    for chunk in range(NT // CHUNK):
        loads[chunk].wait()

        def turn(slot, carry):
            turned[slot] = staged[slot].T
            return carry

        if chunk * CHUNK < NT - FM:
            lax.fori_loop(chunk * CHUNK, (chunk + 1) * CHUNK, turn, 0, unroll=4)

        def halve(slot, carry):
            high, low = split(staged[slot])
            base = pl.multiple_of((slot - (NT - HALVED)) * TILE, TILE)
            weights[pl.ds(base, TILE), 0:TILE] = high
            weights[pl.ds(base, TILE), TILE : 2 * TILE] = low
            return carry

        if chunk * CHUNK >= NT - HALVED:
            lax.fori_loop(chunk * CHUNK, (chunk + 1) * CHUNK, halve, 0, unroll=4)

    var_class = class_ref[...]
    lower = jnp.zeros((CB, TILE), F32)
    upper = jnp.zeros((CB, TILE), F32)
    for class_id in range(lower_ref.shape[1]):
        lower = jnp.where(var_class == class_id, lower_ref[:, class_id : class_id + 1], lower)
        upper = jnp.where(var_class == class_id, upper_ref[:, class_id : class_id + 1], upper)

    first_row = (time - 1) * RB
    first_col = (group * 32 + time) * CB
    slot_id = lax.broadcasted_iota(jnp.int32, (WIN, NT), 1)
    window_id = lax.broadcasted_iota(jnp.int32, (WIN, NT), 0)
    owner_id = window_id // (3 * PIECE)
    block_id = window_id // PIECE - 3 * owner_id
    row_id = block_id * RB + owner_id * PIECE + lax.rem(window_id, PIECE)
    scatter = ((rowv_ref[...] - first_row) == row_id) & (slot_id < count_ref[0])
    gather = ((colv_ref[...] - first_col) == window_id[:CB]) & (slot_id[:CB] < count_ref[0])
    scatter = jnp.where(scatter, 1.0, 0.0)
    chosen = jnp.concatenate([scatter, jnp.where(gather, 1.0, 0.0)], axis=0)
    pick[...] = jnp.concatenate([scatter, scatter], axis=0).astype(BF16)
    if AM:
        last = scatter.T[NT - AM :]
        pick_last[...] = jnp.concatenate([last, last], axis=1).astype(BF16)
    chosen = chosen.astype(BF16)

    def spread(alone):
        width = 8 * (NT - alone) + alone
        lane = lax.broadcasted_iota(jnp.int32, (NT, width), 1)
        owner_slot = jnp.where(lane < 8 * (NT - alone), lane // 8, lane - 7 * (NT - alone))
        hit = owner_slot == lax.broadcasted_iota(jnp.int32, (NT, width), 0)
        return jnp.where(hit, 1.0, 0.0).astype(BF16)

    def twice(value):
        value = value.astype(BF16)
        return jnp.concatenate([value, value], axis=1)

    select_f[...] = twice(jnp.dot(chosen[:WIN], spread(FM), preferred_element_type=F32))
    select_a[...] = twice(
        jnp.dot(chosen[WIN:], spread(0)[:, : 8 * (NT - AM)], preferred_element_type=F32)
    )

    def add_up(select, values):
        high, low = split(values)
        return jnp.dot(select, jnp.concatenate([high, low], axis=0), preferred_element_type=F32)

    def fold(value):
        return jnp.sum(value.reshape(TILE // 8, 8, TILE), axis=0)

    sub_id = lax.broadcasted_iota(jnp.int32, (CB, TILE), 0)

    def adjoint(field):
        field = field[...].reshape(WIN, TILE)
        high, low = split(field.T)
        columns = jnp.dot(
            jnp.concatenate([high, low], axis=1), pick[...], preferred_element_type=F32
        )
        if AM:
            high, low = split(field)
            rows = lax.dot_general(
                pick_last[...],
                jnp.concatenate([high, low], axis=0),
                (((1,), (0,)), ((), ())),
                preferred_element_type=F32,
            )
            for index in range(AM):
                here = sub_id == cols_ref[NT - AM + index] - first_col
                value = rows[index : index + 1]
                high = value.astype(BF16).astype(F32)
                span = slice(index * TILE, (index + 1) * TILE)
                placed[0:CB, span] = jnp.where(here, high, 0.0).astype(BF16)
                placed[CB : 2 * CB, span] = jnp.where(here, value - high, 0.0).astype(BF16)
            total = jnp.dot(placed[...], weights[(HALVED - AM) * TILE :], preferred_element_type=F32)
            total = total[:CB] + total[CB:]
            total = total[:, :TILE] + total[:, TILE:]
        for slot in range(NT - AM):
            factor = jnp.broadcast_to(columns[:, slot : slot + 1], (TILE, TILE))
            partial[8 * slot : 8 * slot + 8] = fold(staged[slot] * factor)
        rest = add_up(select_a[...], partial[0 : 8 * (NT - AM)])
        return total + rest if AM else rest

    def forward(field):
        if FM:
            high, low = split(field)
            halves = jnp.concatenate([high, low], axis=0)
            result = lax.dot_general(
                jnp.concatenate([halves, halves], axis=1),
                weights[(HALVED - FM) * TILE :],
                (((1,), (1,)), ((), ())),
                preferred_element_type=F32,
            )
            for index in range(FM):
                span = slice(index * TILE, (index + 1) * TILE)
                product[index] = result[:CB, span] + result[CB:, span]
        columns = field.T
        for block in range(CB):
            factors[block] = jnp.broadcast_to(columns[:, block : block + 1], (TILE, TILE))
        for slot in range(NT - FM):
            col = jnp.clip(cols_ref[slot] - first_col, 0, CB - 1)
            partial[8 * slot : 8 * slot + 8] = fold(turned[slot] * factors[col])
        for index in range(FM):
            col = jnp.clip(cols_ref[NT - FM + index] - first_col, 0, CB - 1)
            row = 8 * (NT - FM) + index
            partial[row : row + 1] = product[index, pl.ds(col, 1), :]
        return add_up(select_f[...], partial[0 : 8 * (NT - FM) + FM])

    def primal_update(primal, adjoint_part):
        moved = primal - STEP * (cost_ref[...] - adjoint_part)
        return jnp.minimum(jnp.maximum(moved, lower), upper)

    def to_owner(source, target, distance, offset, sems):
        return pltpu.make_async_remote_copy(
            src_ref=source,
            dst_ref=target,
            send_sem=sums_sent.at[sems, distance + 2],
            recv_sem=sums_recv.at[sems, 2 - distance],
            device_id=(owner_group(offset), at(distance)),
            device_id_type=MESH,
        )

    def from_owner(source, target, offset, distance, semaphore):
        return pltpu.make_async_remote_copy(
            src_ref=source,
            dst_ref=target,
            send_sem=send_sems.at[semaphore],
            recv_sem=recv_sems.at[semaphore],
            device_id=(lax.rem(group + offset, 8), at(distance)),
            device_id_type=MESH,
        )

    def rows_of(ref, first, pieces):
        return ref.at[pl.ds(pl.multiple_of(first, PIECE), pieces * PIECE)]

    def copy_a(distance, offset, pieces):
        block = jnp.where(time == NEXT, 0, 1) if distance == 0 else 2 if distance > 0 else 0
        if pieces == 2:
            block = jnp.where(time == NEXT, 0, 1)
        region = {
            0: 0,
            1: jnp.where(time + 1 == NEXT, 2, 4),
            -1: jnp.where(time - 1 == NEXT, 4, 2),
            2: 5,
            -2: 5,
        }[distance]
        if distance == 0 and pieces == 1:
            block = 1
        source = rows_of(terms_a, (owner(offset) * 3 + block) * PIECE, pieces)
        target = rows_of(parts_a, group * SLOT_ROWS + region * PIECE, pieces)
        return to_owner(source, target, distance, offset, 0)

    def copy_b(distance, offset):
        source = rows_of(terms_b, (owner(offset) * 3 + 1 + distance) * PIECE, 1)
        target = rows_of(parts_b, (group * 3 + 1 - distance) * PIECE, 1)
        return to_owner(source, target, distance, offset, 1)

    def to_owners(distance, copy):
        for offset in (1, 0):
            if distance or offset:
                copy(distance, offset).start()
            else:

                @pl.when(jnp.logical_not(is_owner))
                def _():
                    copy(distance, offset).start()

    def steps_a():
        for distance in (1, -1, 0):
            yield distance, exists(distance) & both(distance), 2
        for distance in (1, -1, 0):
            yield distance, exists(distance) & jnp.logical_not(both(distance)), 1

    def wait_rows(semaphore, pieces):
        ref = parts_a.at[0 : pieces * PIECE]
        pltpu.make_async_copy(ref, ref, semaphore).wait()

    def wait_sums_a(semaphores, two_steps, copies, own):
        for distance, when, pieces in steps_a():

            @pl.when(when)
            def _():
                wait_rows(semaphores.at[0, distance + 2], pieces * (copies if distance else own))

        for distance, when in two_steps:

            @pl.when(when)
            def _():
                wait_rows(semaphores.at[0, distance + 2], copies)

    def wait_sums_b(semaphores, copies, own):
        for distance in (1, -1, 0):

            @pl.when(exists(distance))
            def _():
                wait_rows(semaphores.at[1, distance + 2], copies if distance else own)

    for distance, when in ((1, near(1)), (-1, near(-1)), (1, far(1)), (-1, far(-1))):

        @pl.when(when)
        def _():
            dual_in = window_y.at[:, 1 + distance]
            pltpu.make_async_copy(dual_in, dual_in, halo_sems.at[1 + distance]).wait()

            @pl.when(on_core)
            def _():
                pass_on(distance).start()

    primal_0 = x_ref[...]
    primal_1 = primal_update(primal_0, adjoint(window_y))
    terms_a[...] = forward(2.0 * primal_1 - primal_0)
    for distance, when in ((2, time == LAST - 1), (-2, time == NEXT + 1)):

        @pl.when(when)
        def _():
            to_owners(distance, lambda distance, offset: copy_a(distance, offset, 1))

    for distance, when, pieces in steps_a():

        @pl.when(when)
        def _():
            to_owners(distance, lambda distance, offset: copy_a(distance, offset, pieces))

    @pl.when(is_owner)
    def _():
        for pieces, when in ((2, edge), (1, jnp.logical_not(edge))):

            @pl.when(when)
            def _():
                block = jnp.where(time == NEXT, 0, 1) if pieces == 2 else 1
                source = pl.ds(pl.multiple_of((mine * 3 + block) * PIECE, 8), pieces * PIECE)
                target = pl.ds(pl.multiple_of(group * SLOT_ROWS, 8), pieces * PIECE)
                parts_a[target] = terms_a[source]

        for distance in (1, -1):

            @pl.when(far(distance))
            def _():
                rhs_in = window_rhs.at[1 + distance]
                pltpu.make_async_copy(rhs_in, rhs_in, halo_sems.at[2 + distance]).wait()

        wait_sums_a(sums_recv, ((2, time == LAST), (-2, time == NEXT)), 8, 7)
        sums = jnp.sum(parts_a[...].reshape(8, SLOT_ROWS, TILE), axis=0)
        step = [sums[index * PIECE : (index + 1) * PIECE] for index in range(6)]
        low = step[0] + step[2]
        high = step[1] + step[3]
        upper_side = time == NEXT
        first = jnp.where(upper_side, high, low) + step[4]
        second = jnp.where(upper_side, low, high) + step[5]
        for block in range(3):
            image = first if block == 1 else second
            piece_a[block] = jnp.maximum(window_y[mine, block] + STEP * (window_rhs[block] - image), 0.0)
        for distance in (1, -1):

            @pl.when(near(distance))
            def _():
                for offset in range(7, -1, -1):
                    from_owner(
                        piece_a.at[1], window_next.at[mine, 1 - distance], offset, distance, 2 + distance
                    ).start()

        @pl.when(edge)
        def _():
            span = pl.ds(jnp.where(time == NEXT, 0, 1), 2)
            for offset in range(7, 0, -1):
                from_owner(piece_a.at[span], window_next.at[mine, span], offset, 0, 0).start()
            window_next[mine, span] = piece_a[span]

        @pl.when(jnp.logical_not(edge))
        def _():
            for offset in range(7, 0, -1):
                from_owner(piece_a.at[1], window_next.at[mine, 1], offset, 0, 0).start()
            window_next[mine, 1] = piece_a[1]

    for owned, others in ((is_owner, OWN - 1), (jnp.logical_not(is_owner), OWN)):
        for pieces, when in ((2, edge), (1, jnp.logical_not(edge))):

            @pl.when(owned & when)
            def _():
                wait_rows(recv_sems.at[0], pieces * others)

    for distance in (1, -1):

        @pl.when(near(distance))
        def _():
            wait_rows(recv_sems.at[2 - distance], OWN)

    primal_2 = primal_update(primal_1, adjoint(window_next))
    terms_b[...] = forward(2.0 * primal_2 - primal_1)
    for distance in (1, -1, 0):

        @pl.when(exists(distance))
        def _():
            to_owners(distance, copy_b)

    primal_out[0] = primal_1
    primal_out[1] = primal_2
    dual_out[0] = window_next[:, 1]

    @pl.when(is_owner)
    def _():
        own = pl.ds(pl.multiple_of(mine * 3 * PIECE + PIECE, 8), PIECE)
        parts_b[pl.ds(pl.multiple_of(group * 3 * PIECE + PIECE, 8), PIECE)] = terms_b[own]
        wait_sums_b(sums_recv, 8, 7)
        sums = jnp.sum(parts_b[...].reshape(8, 3 * PIECE, TILE), axis=0)
        image = sums[0:PIECE] + sums[PIECE : 2 * PIECE] + sums[2 * PIECE :]
        piece_b[...] = jnp.maximum(piece_a[1] + STEP * (window_rhs[1] - image), 0.0)
        for offset in range(7, 0, -1):
            from_owner(piece_b, last_dual.at[mine], offset, 0, 2).start()
        last_dual[mine] = piece_b[...]
        wait_rows(recv_sems.at[2], OWN - 1)

    @pl.when(jnp.logical_not(is_owner))
    def _():
        wait_rows(recv_sems.at[2], OWN)

    dual_out[1] = last_dual[...]

    for distance in (1, -1):
        for when, copies in dual_copies(distance):

            @pl.when(when)
            def _():
                for copy in copies:
                    copy.wait_send()

    for distance in (1, -1):

        @pl.when(on_core & exists(distance))
        def _():
            pass_on(distance).wait_send()

    two_steps = ((2, time == LAST - 1), (-2, time == NEXT + 1))

    @pl.when(is_owner)
    def _():
        for distance in (1, -1):

            @pl.when(far(distance))
            def _():
                rhs_copy(distance).wait_send()

            @pl.when(near(distance))
            def _():
                wait_rows(send_sems.at[2 + distance], 8)

        wait_sums_a(sums_sent, two_steps, OWN, OWN - 1)
        wait_sums_b(sums_sent, OWN, OWN - 1)
        for pieces, when in ((2, edge), (1, jnp.logical_not(edge))):

            @pl.when(when)
            def _():
                wait_rows(send_sems.at[0], 7 * pieces)

        wait_rows(send_sems.at[2], 7)

    @pl.when(jnp.logical_not(is_owner))
    def _():
        wait_sums_a(sums_sent, two_steps, OWN, OWN)
        wait_sums_b(sums_sent, OWN, OWN)


def means(primals_ref, duals_ref, primal_out, dual_out, primal_mean_out, dual_mean_out):
    for iterates, last, mean in ((primals_ref, primal_out, primal_mean_out), (duals_ref, dual_out, dual_mean_out)):
        last[...] = iterates[1]
        mean[...] = (iterates[0] + iterates[1]) / ITERS


def body(
    x_start,
    y_start,
    cost,
    rhs,
    tiles,
    tile_rows,
    tile_cols,
    tile_count,
    var_class,
    lower_table,
    upper_table,
):
    vmem = pl.BlockSpec(memory_space=pltpu.VMEM)
    primals, duals = pl.pallas_call(
        kernel,
        name="pdhg",
        out_shape=(
            jax.ShapeDtypeStruct((ITERS, CB, TILE), F32),
            jax.ShapeDtypeStruct((ITERS, OWN, PIECE, TILE), F32),
        ),
        in_specs=[pl.BlockSpec(memory_space=pltpu.HBM)] * 12,
        out_specs=(vmem, vmem),
        scratch_shapes=[
            pltpu.VMEM((CB, TILE), F32),
            pltpu.VMEM((OWN, PIECE, TILE), F32),
            pltpu.VMEM((CB, TILE), F32),
            pltpu.VMEM((OWN, PIECE, TILE), F32),
            pltpu.SMEM((NT,), jnp.int32),
            pltpu.SMEM((1,), jnp.int32),
            pltpu.VMEM((1, NT), jnp.int32),
            pltpu.VMEM((1, NT), jnp.int32),
            pltpu.VMEM((CB, TILE), jnp.int32),
            pltpu.VMEM((1, 8), F32),
            pltpu.VMEM((1, 8), F32),
            pltpu.VMEM((NT, TILE, TILE), F32),
            pltpu.VMEM((NT, TILE, TILE), F32),
            pltpu.VMEM((CB, TILE, TILE), F32),
            pltpu.VMEM((max(HALVED, 1) * TILE, 2 * TILE), BF16),
            pltpu.VMEM((2 * CB, max(AM, 1) * TILE), BF16),
            pltpu.VMEM((max(FM, 1), CB, TILE), F32),
            pltpu.VMEM((WIN, 16 * (NT - FM) + 2 * FM), BF16),
            pltpu.VMEM((CB, 16 * (NT - AM)), BF16),
            pltpu.VMEM((8 * NT, TILE), F32),
            pltpu.VMEM((2 * WIN, NT), BF16),
            pltpu.VMEM((max(AM, 1), 2 * WIN), BF16),
            pltpu.VMEM((OWN, 3, PIECE, TILE), F32),
            pltpu.VMEM((3, PIECE, TILE), F32),
            pltpu.VMEM((OWN, 3, PIECE, TILE), F32),
            pltpu.VMEM((WIN, TILE), F32),
            pltpu.VMEM((WIN, TILE), F32),
            pltpu.VMEM((8 * SLOT_ROWS, TILE), F32),
            pltpu.VMEM((8 * 3 * PIECE, TILE), F32),
            pltpu.VMEM((3, PIECE, TILE), F32),
            pltpu.VMEM((PIECE, TILE), F32),
            pltpu.VMEM((OWN, PIECE, TILE), F32),
            pltpu.SemaphoreType.DMA((NT // CHUNK,)),
            pltpu.SemaphoreType.DMA((11,)),
            pltpu.SemaphoreType.DMA((8,)),
            pltpu.SemaphoreType.DMA((8,)),
            pltpu.SemaphoreType.DMA((2, 5)),
            pltpu.SemaphoreType.DMA((2, 5)),
            pltpu.SemaphoreType.DMA((4,)),
            pltpu.SemaphoreType.DMA((4,)),
        ],
        compiler_params=pltpu.CompilerParams(
            collective_id=0, has_side_effects=True, vmem_limit_bytes=60 * 1024 * 1024
        ),
    )(
        x_start,
        y_start.reshape(OWN, PIECE, TILE),
        cost,
        rhs.reshape(OWN, PIECE, TILE),
        tiles,
        tile_cols,
        tile_count,
        tile_rows.reshape(1, NT),
        tile_cols.reshape(1, NT),
        var_class,
        lower_table.reshape(1, 8),
        upper_table.reshape(1, 8),
    )
    columns = jax.ShapeDtypeStruct((CB, TILE), F32)
    rows = jax.ShapeDtypeStruct((RB, TILE), F32)
    return pl.pallas_call(
        means,
        name="means",
        out_shape=(columns, rows, columns, rows),
        in_specs=[vmem, vmem],
        out_specs=(vmem, vmem, vmem, vmem),
    )(primals, duals.reshape(ITERS, RB, TILE))


def solution(mesh):
    return jax.shard_map(
        body,
        mesh=mesh,
        in_specs=(
            P(("grp", "tm"), None),
            P("tm", None),
            P(("grp", "tm"), None),
            P("tm", None),
            P(("grp", "tm"), None, None),
            P(("grp", "tm")),
            P(("grp", "tm")),
            P(("grp", "tm")),
            P(("grp", "tm"), None),
            P(),
            P(),
        ),
        out_specs=(P(("grp", "tm"), None), P("tm", None), P(("grp", "tm"), None), P("tm", None)),
        check_vma=False,
    )
```

```python
import jax
import jax.numpy as jnp
from jax import lax
from jax.experimental import pallas as pl
from jax.experimental.pallas import tpu as pltpu
from jax.sharding import PartitionSpec as P

ITERS = 2
STEP = 0.6
MESH = pl.DeviceIdType.MESH
F32 = jnp.float32
BF16 = jnp.bfloat16

NT = 64
TILE = 128
CB = 16
RB = 32
OWN = 2
PIECE = RB // OWN
WIN = 3 * RB
CHUNK = 8
AM = 24
FM = 16
HALVED = max(AM, FM)

LAST, NEXT = 15, 16
SLOT_ROWS = 6 * PIECE


def split(value):
    high = value.astype(BF16)
    return high, (value - high.astype(F32)).astype(BF16)


def kernel(
    x_hbm,
    y_hbm,
    cost_hbm,
    rhs_hbm,
    tiles_hbm,
    cols_hbm,
    count_hbm,
    rowv_hbm,
    colv_hbm,
    class_hbm,
    lower_hbm,
    upper_hbm,
    primal_out,
    dual_out,
    x_ref,
    y_ref,
    cost_ref,
    rhs_ref,
    cols_ref,
    count_ref,
    rowv_ref,
    colv_ref,
    class_ref,
    lower_ref,
    upper_ref,
    staged,
    turned,
    factors,
    weights,
    placed,
    product,
    select_f,
    select_a,
    partial,
    pick,
    pick_last,
    window_y,
    window_rhs,
    window_next,
    terms_a,
    terms_b,
    parts_a,
    parts_b,
    piece_a,
    piece_b,
    last_dual,
    load_sem,
    input_sems,
    dual_sems,
    halo_sems,
    sums_sent,
    sums_recv,
    send_sems,
    recv_sems,
):
    group = lax.axis_index("grp")
    time = lax.axis_index("tm")
    place = group // 2
    core = lax.rem(group, 2)
    on_core = core == 1
    is_owner = on_core & ((place == 1) | (place == 2))
    mine = place // 2

    def at(distance):
        return time + distance

    def exists(distance):
        there = time + distance
        return (there >= 0) & (there < 32)

    def number(distances):
        return sum(jnp.where(exists(distance), 1, 0) for distance in distances)

    def owner(offset):
        return lax.rem(mine + offset, OWN)

    def owner_group(offset):
        return 2 * owner(offset) + 3

    def far(distance):
        return (time == LAST) if distance > 0 else (time == NEXT)

    def near(distance):
        return exists(distance) & jnp.logical_not(far(distance))

    edge = (time == LAST) | (time == NEXT)
    at_end = (place == 0) | (place == 3)

    def both(distance):
        return edge if distance == 0 else far(distance)

    window_rhs[...] = jnp.zeros_like(window_rhs)

    @pl.when(jnp.logical_not(edge))
    def _():
        parts_a[...] = jnp.zeros_like(parts_a)

    @pl.when((time == 0) | (time == 31))
    def _():
        parts_b[...] = jnp.zeros_like(parts_b)
        window_y[...] = jnp.zeros_like(window_y)
        window_next[...] = jnp.zeros_like(window_next)

    barrier = pltpu.get_barrier_semaphore()

    def greet(target_group, target_time):
        pl.semaphore_signal(
            barrier, inc=1, device_id=(target_group, target_time), device_id_type=MESH
        )

    def greet_all(distance):
        for offset in range(7, -1, -1):
            if distance or offset:
                greet(lax.rem(group + offset, 8), at(distance))

    source_place = jnp.where(place >= 2, 0, 3)
    left = jnp.where(place == 3, 0, 2)

    @pl.when(is_owner)
    def _():
        for distance, when in ((2, time == LAST), (-2, time == NEXT), (1, exists(1)), (-1, exists(-1))):

            @pl.when(when)
            def _():
                greet_all(distance)

        greet_all(0)

    @pl.when(jnp.logical_not(is_owner))
    def _():
        for distance in (1, -1):

            @pl.when(on_core & far(distance))
            def _():
                greet(2 * source_place + 1, at(distance))

            @pl.when(on_core & near(distance))
            def _():
                greet(group, at(distance))

            @pl.when(near(distance))
            def _():
                for offset in range(OWN):
                    greet(owner_group(offset), at(distance))

        for offset in range(OWN):
            greet(owner_group(offset), time)

        @pl.when(jnp.logical_not(on_core) & at_end)
        def _():
            greet(group + 1, time)

    inputs = []
    for index, (source, target) in enumerate(
        (
            (y_hbm, y_ref),
            (rhs_hbm, rhs_ref),
            (x_hbm, x_ref),
            (cost_hbm, cost_ref),
            (class_hbm, class_ref),
            (rowv_hbm, rowv_ref),
            (colv_hbm, colv_ref),
            (count_hbm, count_ref),
            (lower_hbm, lower_ref),
            (upper_hbm, upper_ref),
            (cols_hbm, cols_ref),
        )
    ):
        copy = pltpu.make_async_copy(source, target, input_sems.at[index])
        copy.start()
        inputs.append(copy)
    loads = []
    for chunk in range(NT // CHUNK):
        span = pl.ds(chunk * CHUNK, CHUNK)
        load = pltpu.make_async_copy(tiles_hbm.at[span], staged.at[span], load_sem.at[chunk])
        load.start()
        loads.append(load)
    for copy in inputs:
        copy.wait()

    of_owner = 7
    for distance in (1, -1):
        of_owner = of_owner + jnp.where(near(distance), 8, 0)
        of_owner = of_owner + jnp.where(far(distance), OWN, 0)
    two_steps = jnp.where((time == LAST - 1) | (time == NEXT + 1), OWN, 0)
    of_other = OWN * number((1, 0, -1))
    of_sender = of_other + number((1, -1)) + 1
    peers = jnp.where(is_owner, of_owner, jnp.where(on_core, of_sender, of_other))
    pl.semaphore_wait(barrier, peers + two_steps)

    def dual_copies(distance):
        slot = 1 - distance

        def copy(target, number):
            return pltpu.make_async_remote_copy(
                src_ref=y_ref,
                dst_ref=window_y.at[:, slot],
                send_sem=dual_sems.at[slot // 2 * 4 + number],
                recv_sem=halo_sems.at[slot],
                device_id=(2 * target + 1, at(distance)),
                device_id_type=MESH,
            )

        return [
            (on_core & far(distance) & at_end, [copy(left, 0), copy(left + 1, 1)]),
            (on_core & near(distance), [copy(place, 2)]),
        ]

    def pass_on(distance):
        slot = 1 + distance
        return pltpu.make_async_remote_copy(
            src_ref=window_y.at[:, slot],
            dst_ref=window_y.at[:, slot],
            send_sem=dual_sems.at[slot // 2 * 4 + 3],
            recv_sem=halo_sems.at[slot],
            device_id=(group - 1, time),
            device_id_type=MESH,
        )

    def rhs_copy(distance):
        slot = 1 - distance
        return pltpu.make_async_remote_copy(
            src_ref=rhs_ref.at[mine],
            dst_ref=window_rhs.at[slot],
            send_sem=halo_sems.at[slot + 4],
            recv_sem=halo_sems.at[slot + 1],
            device_id=(group, at(distance)),
            device_id_type=MESH,
        )

    for distance in (1, -1):
        for when, copies in dual_copies(distance):

            @pl.when(when)
            def _():
                for copy in copies:
                    copy.start()

    @pl.when(is_owner)
    def _():
        for distance in (1, -1):

            @pl.when(far(distance))
            def _():
                rhs_copy(distance).start()

    window_y[:, 1] = y_ref[...]
    window_rhs[1] = rhs_ref[mine]

    for chunk in range(NT // CHUNK):
        loads[chunk].wait()

        def turn(slot, carry):
            turned[slot] = staged[slot].T
            return carry

        if chunk * CHUNK < NT - FM:
            lax.fori_loop(chunk * CHUNK, (chunk + 1) * CHUNK, turn, 0, unroll=4)

        def halve(slot, carry):
            high, low = split(staged[slot])
            base = pl.multiple_of((slot - (NT - HALVED)) * TILE, TILE)
            weights[pl.ds(base, TILE), 0:TILE] = high
            weights[pl.ds(base, TILE), TILE : 2 * TILE] = low
            return carry

        if chunk * CHUNK >= NT - HALVED:
            lax.fori_loop(chunk * CHUNK, (chunk + 1) * CHUNK, halve, 0, unroll=4)

    var_class = class_ref[...]
    lower = jnp.zeros((CB, TILE), F32)
    upper = jnp.zeros((CB, TILE), F32)
    for class_id in range(lower_ref.shape[1]):
        lower = jnp.where(var_class == class_id, lower_ref[:, class_id : class_id + 1], lower)
        upper = jnp.where(var_class == class_id, upper_ref[:, class_id : class_id + 1], upper)

    first_row = (time - 1) * RB
    first_col = (group * 32 + time) * CB
    slot_id = lax.broadcasted_iota(jnp.int32, (WIN, NT), 1)
    window_id = lax.broadcasted_iota(jnp.int32, (WIN, NT), 0)
    owner_id = window_id // (3 * PIECE)
    block_id = window_id // PIECE - 3 * owner_id
    row_id = block_id * RB + owner_id * PIECE + lax.rem(window_id, PIECE)
    scatter = ((rowv_ref[...] - first_row) == row_id) & (slot_id < count_ref[0])
    gather = ((colv_ref[...] - first_col) == window_id[:CB]) & (slot_id[:CB] < count_ref[0])
    scatter = jnp.where(scatter, 1.0, 0.0)
    chosen = jnp.concatenate([scatter, jnp.where(gather, 1.0, 0.0)], axis=0)
    pick[...] = jnp.concatenate([scatter, scatter], axis=0).astype(BF16)
    if AM:
        last = scatter.T[NT - AM :]
        pick_last[...] = jnp.concatenate([last, last], axis=1).astype(BF16)
    chosen = chosen.astype(BF16)

    def spread(alone):
        width = 8 * (NT - alone) + alone
        lane = lax.broadcasted_iota(jnp.int32, (NT, width), 1)
        owner_slot = jnp.where(lane < 8 * (NT - alone), lane // 8, lane - 7 * (NT - alone))
        hit = owner_slot == lax.broadcasted_iota(jnp.int32, (NT, width), 0)
        return jnp.where(hit, 1.0, 0.0).astype(BF16)

    def twice(value):
        value = value.astype(BF16)
        return jnp.concatenate([value, value], axis=1)

    select_f[...] = twice(jnp.dot(chosen[:WIN], spread(FM), preferred_element_type=F32))
    select_a[...] = twice(
        jnp.dot(chosen[WIN:], spread(0)[:, : 8 * (NT - AM)], preferred_element_type=F32)
    )

    def add_up(select, values):
        high, low = split(values)
        return jnp.dot(select, jnp.concatenate([high, low], axis=0), preferred_element_type=F32)

    def fold(value):
        return jnp.sum(value.reshape(TILE // 8, 8, TILE), axis=0)

    sub_id = lax.broadcasted_iota(jnp.int32, (CB, TILE), 0)

    def adjoint(field):
        field = field[...].reshape(WIN, TILE)
        high, low = split(field.T)
        columns = jnp.dot(
            jnp.concatenate([high, low], axis=1), pick[...], preferred_element_type=F32
        )
        if AM:
            high, low = split(field)
            rows = lax.dot_general(
                pick_last[...],
                jnp.concatenate([high, low], axis=0),
                (((1,), (0,)), ((), ())),
                preferred_element_type=F32,
            )
            for index in range(AM):
                here = sub_id == cols_ref[NT - AM + index] - first_col
                value = rows[index : index + 1]
                high = value.astype(BF16).astype(F32)
                span = slice(index * TILE, (index + 1) * TILE)
                placed[0:CB, span] = jnp.where(here, high, 0.0).astype(BF16)
                placed[CB : 2 * CB, span] = jnp.where(here, value - high, 0.0).astype(BF16)
            total = jnp.dot(placed[...], weights[(HALVED - AM) * TILE :], preferred_element_type=F32)
            total = total[:CB] + total[CB:]
            total = total[:, :TILE] + total[:, TILE:]
        for slot in range(NT - AM):
            factor = jnp.broadcast_to(columns[:, slot : slot + 1], (TILE, TILE))
            partial[8 * slot : 8 * slot + 8] = fold(staged[slot] * factor)
        rest = add_up(select_a[...], partial[0 : 8 * (NT - AM)])
        return total + rest if AM else rest

    def forward(field):
        if FM:
            high, low = split(field)
            halves = jnp.concatenate([high, low], axis=0)
            result = lax.dot_general(
                jnp.concatenate([halves, halves], axis=1),
                weights[(HALVED - FM) * TILE :],
                (((1,), (1,)), ((), ())),
                preferred_element_type=F32,
            )
            for index in range(FM):
                span = slice(index * TILE, (index + 1) * TILE)
                product[index] = result[:CB, span] + result[CB:, span]
        columns = field.T
        for block in range(CB):
            factors[block] = jnp.broadcast_to(columns[:, block : block + 1], (TILE, TILE))
        for slot in range(NT - FM):
            col = jnp.clip(cols_ref[slot] - first_col, 0, CB - 1)
            partial[8 * slot : 8 * slot + 8] = fold(turned[slot] * factors[col])
        for index in range(FM):
            col = jnp.clip(cols_ref[NT - FM + index] - first_col, 0, CB - 1)
            row = 8 * (NT - FM) + index
            partial[row : row + 1] = product[index, pl.ds(col, 1), :]
        return add_up(select_f[...], partial[0 : 8 * (NT - FM) + FM])

    def primal_update(primal, adjoint_part):
        moved = primal - STEP * (cost_ref[...] - adjoint_part)
        return jnp.minimum(jnp.maximum(moved, lower), upper)

    def to_owner(source, target, distance, offset, sems):
        return pltpu.make_async_remote_copy(
            src_ref=source,
            dst_ref=target,
            send_sem=sums_sent.at[sems, distance + 2],
            recv_sem=sums_recv.at[sems, 2 - distance],
            device_id=(owner_group(offset), at(distance)),
            device_id_type=MESH,
        )

    def from_owner(source, target, offset, distance, semaphore):
        return pltpu.make_async_remote_copy(
            src_ref=source,
            dst_ref=target,
            send_sem=send_sems.at[semaphore],
            recv_sem=recv_sems.at[semaphore],
            device_id=(lax.rem(group + offset, 8), at(distance)),
            device_id_type=MESH,
        )

    def rows_of(ref, first, pieces):
        return ref.at[pl.ds(pl.multiple_of(first, PIECE), pieces * PIECE)]

    def copy_a(distance, offset, pieces):
        block = jnp.where(time == NEXT, 0, 1) if distance == 0 else 2 if distance > 0 else 0
        if pieces == 2:
            block = jnp.where(time == NEXT, 0, 1)
        region = {
            0: 0,
            1: jnp.where(time + 1 == NEXT, 2, 4),
            -1: jnp.where(time - 1 == NEXT, 4, 2),
            2: 5,
            -2: 5,
        }[distance]
        if distance == 0 and pieces == 1:
            block = 1
        source = rows_of(terms_a, (owner(offset) * 3 + block) * PIECE, pieces)
        target = rows_of(parts_a, group * SLOT_ROWS + region * PIECE, pieces)
        return to_owner(source, target, distance, offset, 0)

    def copy_b(distance, offset):
        source = rows_of(terms_b, (owner(offset) * 3 + 1 + distance) * PIECE, 1)
        target = rows_of(parts_b, (group * 3 + 1 - distance) * PIECE, 1)
        return to_owner(source, target, distance, offset, 1)

    def to_owners(distance, copy):
        for offset in (1, 0):
            if distance or offset:
                copy(distance, offset).start()
            else:

                @pl.when(jnp.logical_not(is_owner))
                def _():
                    copy(distance, offset).start()

    def steps_a():
        for distance in (1, -1, 0):
            yield distance, exists(distance) & both(distance), 2
        for distance in (1, -1, 0):
            yield distance, exists(distance) & jnp.logical_not(both(distance)), 1

    def wait_rows(semaphore, pieces):
        ref = parts_a.at[0 : pieces * PIECE]
        pltpu.make_async_copy(ref, ref, semaphore).wait()

    def wait_sums_a(semaphores, two_steps, copies, own):
        for distance, when, pieces in steps_a():

            @pl.when(when)
            def _():
                wait_rows(semaphores.at[0, distance + 2], pieces * (copies if distance else own))

        for distance, when in two_steps:

            @pl.when(when)
            def _():
                wait_rows(semaphores.at[0, distance + 2], copies)

    def wait_sums_b(semaphores, copies, own):
        for distance in (1, -1, 0):

            @pl.when(exists(distance))
            def _():
                wait_rows(semaphores.at[1, distance + 2], copies if distance else own)

    for distance, when in ((1, near(1)), (-1, near(-1)), (1, far(1)), (-1, far(-1))):

        @pl.when(when)
        def _():
            dual_in = window_y.at[:, 1 + distance]
            pltpu.make_async_copy(dual_in, dual_in, halo_sems.at[1 + distance]).wait()

            @pl.when(on_core)
            def _():
                pass_on(distance).start()

    primal_0 = x_ref[...]
    primal_1 = primal_update(primal_0, adjoint(window_y))
    terms_a[...] = forward(2.0 * primal_1 - primal_0)
    for distance, when in ((2, time == LAST - 1), (-2, time == NEXT + 1)):

        @pl.when(when)
        def _():
            to_owners(distance, lambda distance, offset: copy_a(distance, offset, 1))

    for distance, when, pieces in steps_a():

        @pl.when(when)
        def _():
            to_owners(distance, lambda distance, offset: copy_a(distance, offset, pieces))

    @pl.when(is_owner)
    def _():
        for pieces, when in ((2, edge), (1, jnp.logical_not(edge))):

            @pl.when(when)
            def _():
                block = jnp.where(time == NEXT, 0, 1) if pieces == 2 else 1
                source = pl.ds(pl.multiple_of((mine * 3 + block) * PIECE, 8), pieces * PIECE)
                target = pl.ds(pl.multiple_of(group * SLOT_ROWS, 8), pieces * PIECE)
                parts_a[target] = terms_a[source]

        def summed(ref, stride, first):
            return sum(
                ref[pl.ds(pl.multiple_of((index * stride + first) * PIECE, PIECE), PIECE)] for index in range(8)
            )

        for distance, when, pieces in steps_a():

            @pl.when(when & jnp.logical_not(far(distance) if distance else False))
            def _():
                wait_rows(sums_recv.at[0, distance + 2], pieces * (8 if distance else 7))

        early = [summed(parts_a, 6, index) for index in (0, 1, 4)]
        for distance in (1, -1):

            @pl.when(far(distance))
            def _():
                rhs_in = window_rhs.at[1 + distance]
                pltpu.make_async_copy(rhs_in, rhs_in, halo_sems.at[2 + distance]).wait()
                wait_rows(sums_recv.at[0, distance + 2], 2 * 8)

        for distance, when in ((2, time == LAST), (-2, time == NEXT)):

            @pl.when(when)
            def _():
                wait_rows(sums_recv.at[0, distance + 2], 8)

        step = [early[0], early[1], summed(parts_a, 6, 2), summed(parts_a, 6, 3), early[2], summed(parts_a, 6, 5)]
        low = step[0] + step[2]
        high = step[1] + step[3]
        upper_side = time == NEXT
        first = jnp.where(upper_side, high, low) + step[4]
        second = jnp.where(upper_side, low, high) + step[5]
        for block in range(3):
            image = first if block == 1 else second
            piece_a[block] = jnp.maximum(window_y[mine, block] + STEP * (window_rhs[block] - image), 0.0)
        @pl.when(edge)
        def _():
            span = pl.ds(jnp.where(time == NEXT, 0, 1), 2)
            for offset in (3, 5, 1, 7, 4, 2, 6):
                from_owner(piece_a.at[span], window_next.at[mine, span], offset, 0, 0).start()
            window_next[mine, span] = piece_a[span]

        @pl.when(jnp.logical_not(edge))
        def _():
            for offset in (3, 5, 1, 7, 4, 2, 6):
                from_owner(piece_a.at[1], window_next.at[mine, 1], offset, 0, 0).start()
            window_next[mine, 1] = piece_a[1]

        for distance in (1, -1):

            @pl.when(near(distance))
            def _():
                for offset in range(7, -1, -1):
                    from_owner(
                        piece_a.at[1], window_next.at[mine, 1 - distance], offset, distance, 2 + distance
                    ).start()

    for owned, others in ((is_owner, OWN - 1), (jnp.logical_not(is_owner), OWN)):
        for pieces, when in ((2, edge), (1, jnp.logical_not(edge))):

            @pl.when(owned & when)
            def _():
                wait_rows(recv_sems.at[0], pieces * others)

    for distance in (1, -1):

        @pl.when(near(distance))
        def _():
            wait_rows(recv_sems.at[2 - distance], OWN)

    primal_2 = primal_update(primal_1, adjoint(window_next))
    terms_b[...] = forward(2.0 * primal_2 - primal_1)
    for distance in (1, -1, 0):

        @pl.when(exists(distance))
        def _():
            to_owners(distance, copy_b)

    primal_out[0] = primal_1
    primal_out[1] = primal_2
    dual_out[0] = window_next[:, 1]

    @pl.when(is_owner)
    def _():
        own = pl.ds(pl.multiple_of(mine * 3 * PIECE + PIECE, 8), PIECE)
        parts_b[pl.ds(pl.multiple_of(group * 3 * PIECE + PIECE, 8), PIECE)] = terms_b[own]
        def summed(first):
            return sum(
                parts_b[pl.ds(pl.multiple_of((index * 3 + first) * PIECE, PIECE), PIECE)] for index in range(8)
            )

        wait_rows(sums_recv.at[1, 2], 7)
        for distance in (1, -1):

            @pl.when(near(distance))
            def _():
                wait_rows(sums_recv.at[1, distance + 2], 8)

        near_block = jnp.where(time == LAST, 0, 2)
        early = summed(1) + summed(near_block)
        for distance in (1, -1):

            @pl.when(far(distance))
            def _():
                wait_rows(sums_recv.at[1, distance + 2], 8)

        image = early + summed(2 - near_block)
        piece_b[...] = jnp.maximum(piece_a[1] + STEP * (window_rhs[1] - image), 0.0)
        for offset in (3, 5, 1, 7, 4, 2, 6):
            from_owner(piece_b, last_dual.at[mine], offset, 0, 2).start()
        last_dual[mine] = piece_b[...]
        wait_rows(recv_sems.at[2], OWN - 1)

    @pl.when(jnp.logical_not(is_owner))
    def _():
        wait_rows(recv_sems.at[2], OWN)

    dual_out[1] = last_dual[...]

    for distance in (1, -1):
        for when, copies in dual_copies(distance):

            @pl.when(when)
            def _():
                for copy in copies:
                    copy.wait_send()

    for distance in (1, -1):

        @pl.when(on_core & exists(distance))
        def _():
            pass_on(distance).wait_send()

    two_steps = ((2, time == LAST - 1), (-2, time == NEXT + 1))

    @pl.when(is_owner)
    def _():
        for distance in (1, -1):

            @pl.when(far(distance))
            def _():
                rhs_copy(distance).wait_send()

            @pl.when(near(distance))
            def _():
                wait_rows(send_sems.at[2 + distance], 8)

        wait_sums_a(sums_sent, two_steps, OWN, OWN - 1)
        wait_sums_b(sums_sent, OWN, OWN - 1)
        for pieces, when in ((2, edge), (1, jnp.logical_not(edge))):

            @pl.when(when)
            def _():
                wait_rows(send_sems.at[0], 7 * pieces)

        wait_rows(send_sems.at[2], 7)

    @pl.when(jnp.logical_not(is_owner))
    def _():
        wait_sums_a(sums_sent, two_steps, OWN, OWN)
        wait_sums_b(sums_sent, OWN, OWN)


def means(primals_ref, duals_ref, primal_out, dual_out, primal_mean_out, dual_mean_out):
    for iterates, last, mean in ((primals_ref, primal_out, primal_mean_out), (duals_ref, dual_out, dual_mean_out)):
        last[...] = iterates[1]
        mean[...] = (iterates[0] + iterates[1]) / ITERS


def body(
    x_start,
    y_start,
    cost,
    rhs,
    tiles,
    tile_rows,
    tile_cols,
    tile_count,
    var_class,
    lower_table,
    upper_table,
):
    vmem = pl.BlockSpec(memory_space=pltpu.VMEM)
    primals, duals = pl.pallas_call(
        kernel,
        name="pdhg",
        out_shape=(
            jax.ShapeDtypeStruct((ITERS, CB, TILE), F32),
            jax.ShapeDtypeStruct((ITERS, OWN, PIECE, TILE), F32),
        ),
        in_specs=[pl.BlockSpec(memory_space=pltpu.HBM)] * 12,
        out_specs=(vmem, vmem),
        scratch_shapes=[
            pltpu.VMEM((CB, TILE), F32),
            pltpu.VMEM((OWN, PIECE, TILE), F32),
            pltpu.VMEM((CB, TILE), F32),
            pltpu.VMEM((OWN, PIECE, TILE), F32),
            pltpu.SMEM((NT,), jnp.int32),
            pltpu.SMEM((1,), jnp.int32),
            pltpu.VMEM((1, NT), jnp.int32),
            pltpu.VMEM((1, NT), jnp.int32),
            pltpu.VMEM((CB, TILE), jnp.int32),
            pltpu.VMEM((1, 8), F32),
            pltpu.VMEM((1, 8), F32),
            pltpu.VMEM((NT, TILE, TILE), F32),
            pltpu.VMEM((NT, TILE, TILE), F32),
            pltpu.VMEM((CB, TILE, TILE), F32),
            pltpu.VMEM((max(HALVED, 1) * TILE, 2 * TILE), BF16),
            pltpu.VMEM((2 * CB, max(AM, 1) * TILE), BF16),
            pltpu.VMEM((max(FM, 1), CB, TILE), F32),
            pltpu.VMEM((WIN, 16 * (NT - FM) + 2 * FM), BF16),
            pltpu.VMEM((CB, 16 * (NT - AM)), BF16),
            pltpu.VMEM((8 * NT, TILE), F32),
            pltpu.VMEM((2 * WIN, NT), BF16),
            pltpu.VMEM((max(AM, 1), 2 * WIN), BF16),
            pltpu.VMEM((OWN, 3, PIECE, TILE), F32),
            pltpu.VMEM((3, PIECE, TILE), F32),
            pltpu.VMEM((OWN, 3, PIECE, TILE), F32),
            pltpu.VMEM((WIN, TILE), F32),
            pltpu.VMEM((WIN, TILE), F32),
            pltpu.VMEM((8 * SLOT_ROWS, TILE), F32),
            pltpu.VMEM((8 * 3 * PIECE, TILE), F32),
            pltpu.VMEM((3, PIECE, TILE), F32),
            pltpu.VMEM((PIECE, TILE), F32),
            pltpu.VMEM((OWN, PIECE, TILE), F32),
            pltpu.SemaphoreType.DMA((NT // CHUNK,)),
            pltpu.SemaphoreType.DMA((11,)),
            pltpu.SemaphoreType.DMA((8,)),
            pltpu.SemaphoreType.DMA((8,)),
            pltpu.SemaphoreType.DMA((2, 5)),
            pltpu.SemaphoreType.DMA((2, 5)),
            pltpu.SemaphoreType.DMA((4,)),
            pltpu.SemaphoreType.DMA((4,)),
        ],
        compiler_params=pltpu.CompilerParams(
            collective_id=0, has_side_effects=True, vmem_limit_bytes=60 * 1024 * 1024
        ),
    )(
        x_start,
        y_start.reshape(OWN, PIECE, TILE),
        cost,
        rhs.reshape(OWN, PIECE, TILE),
        tiles,
        tile_cols,
        tile_count,
        tile_rows.reshape(1, NT),
        tile_cols.reshape(1, NT),
        var_class,
        lower_table.reshape(1, 8),
        upper_table.reshape(1, 8),
    )
    columns = jax.ShapeDtypeStruct((CB, TILE), F32)
    rows = jax.ShapeDtypeStruct((RB, TILE), F32)
    return pl.pallas_call(
        means,
        name="means",
        out_shape=(columns, rows, columns, rows),
        in_specs=[vmem, vmem],
        out_specs=(vmem, vmem, vmem, vmem),
    )(primals, duals.reshape(ITERS, RB, TILE))


def solution(mesh):
    return jax.shard_map(
        body,
        mesh=mesh,
        in_specs=(
            P(("grp", "tm"), None),
            P("tm", None),
            P(("grp", "tm"), None),
            P("tm", None),
            P(("grp", "tm"), None, None),
            P(("grp", "tm")),
            P(("grp", "tm")),
            P(("grp", "tm")),
            P(("grp", "tm"), None),
            P(),
            P(),
        ),
        out_specs=(P(("grp", "tm"), None), P("tm", None), P(("grp", "tm"), None), P("tm", None)),
        check_vma=False,
    )
```

```python
import jax
import jax.numpy as jnp
from jax import lax
from jax.experimental import pallas as pl
from jax.experimental.pallas import tpu as pltpu
from jax.sharding import PartitionSpec as P

ITERS = 2
STEP = 0.6
MESH = pl.DeviceIdType.MESH
F32 = jnp.float32
BF16 = jnp.bfloat16

NT = 64
TILE = 128
CB = 16
RB = 32
OWN = 2
PIECE = RB // OWN
WIN = 3 * RB
CHUNK = 8
AM = 24
FM = 16
HALVED = max(AM, FM)

LAST, NEXT = 15, 16
SLOT_ROWS = 6 * PIECE


def split(value):
    high = value.astype(BF16)
    return high, (value - high.astype(F32)).astype(BF16)


def kernel(
    x_hbm,
    y_hbm,
    cost_hbm,
    rhs_hbm,
    tiles_hbm,
    cols_hbm,
    count_hbm,
    rowv_hbm,
    colv_hbm,
    class_hbm,
    lower_hbm,
    upper_hbm,
    primal_out,
    dual_out,
    x_ref,
    y_ref,
    cost_ref,
    rhs_ref,
    cols_ref,
    count_ref,
    rowv_ref,
    colv_ref,
    class_ref,
    lower_ref,
    upper_ref,
    staged,
    turned,
    factors,
    weights,
    placed,
    product,
    select_f,
    select_a,
    partial,
    pick,
    pick_last,
    window_y,
    window_rhs,
    window_next,
    terms_a,
    terms_b,
    parts_a,
    parts_b,
    piece_a,
    piece_b,
    primals,
    load_sem,
    out_sems,
    input_sems,
    dual_sems,
    halo_sems,
    sums_sent,
    sums_recv,
    send_sems,
    recv_sems,
):
    group = lax.axis_index("grp")
    time = lax.axis_index("tm")
    place = group // 2
    core = lax.rem(group, 2)
    on_core = core == 1
    is_owner = on_core & ((place == 1) | (place == 2))
    mine = place // 2

    def at(distance):
        return time + distance

    def exists(distance):
        there = time + distance
        return (there >= 0) & (there < 32)

    def number(distances):
        return sum(jnp.where(exists(distance), 1, 0) for distance in distances)

    def owner(offset):
        return lax.rem(mine + offset, OWN)

    def owner_group(offset):
        return 2 * owner(offset) + 3

    def far(distance):
        return (time == LAST) if distance > 0 else (time == NEXT)

    def near(distance):
        return exists(distance) & jnp.logical_not(far(distance))

    edge = (time == LAST) | (time == NEXT)
    at_end = (place == 0) | (place == 3)

    def both(distance):
        return edge if distance == 0 else far(distance)

    window_rhs[...] = jnp.zeros_like(window_rhs)

    @pl.when(jnp.logical_not(edge))
    def _():
        parts_a[...] = jnp.zeros_like(parts_a)

    @pl.when((time == 0) | (time == 31))
    def _():
        parts_b[...] = jnp.zeros_like(parts_b)
        window_y[...] = jnp.zeros_like(window_y)
        window_next[...] = jnp.zeros_like(window_next)

    barrier = pltpu.get_barrier_semaphore()

    def greet(target_group, target_time):
        pl.semaphore_signal(
            barrier, inc=1, device_id=(target_group, target_time), device_id_type=MESH
        )

    def greet_all(distance):
        for offset in range(7, -1, -1):
            if distance or offset:
                greet(lax.rem(group + offset, 8), at(distance))

    source_place = jnp.where(place >= 2, 0, 3)
    left = jnp.where(place == 3, 0, 2)

    @pl.when(is_owner)
    def _():
        for distance, when in ((2, time == LAST), (-2, time == NEXT), (1, exists(1)), (-1, exists(-1))):

            @pl.when(when)
            def _():
                greet_all(distance)

        greet_all(0)

    @pl.when(jnp.logical_not(is_owner))
    def _():
        for distance in (1, -1):

            @pl.when(on_core & far(distance))
            def _():
                greet(2 * source_place + 1, at(distance))

            @pl.when(on_core & near(distance))
            def _():
                greet(group, at(distance))

            @pl.when(near(distance))
            def _():
                for offset in range(OWN):
                    greet(owner_group(offset), at(distance))

        for offset in range(OWN):
            greet(owner_group(offset), time)

        @pl.when(jnp.logical_not(on_core) & at_end)
        def _():
            greet(group + 1, time)

    inputs = []
    for index, (source, target) in enumerate(
        (
            (y_hbm, y_ref),
            (rhs_hbm, rhs_ref),
            (x_hbm, x_ref),
            (cost_hbm, cost_ref),
            (class_hbm, class_ref),
            (rowv_hbm, rowv_ref),
            (colv_hbm, colv_ref),
            (count_hbm, count_ref),
            (lower_hbm, lower_ref),
            (upper_hbm, upper_ref),
            (cols_hbm, cols_ref),
        )
    ):
        copy = pltpu.make_async_copy(source, target, input_sems.at[index])
        copy.start()
        inputs.append(copy)
    loads = []
    for chunk in range(NT // CHUNK):
        span = pl.ds(chunk * CHUNK, CHUNK)
        load = pltpu.make_async_copy(tiles_hbm.at[span], staged.at[span], load_sem.at[chunk])
        load.start()
        loads.append(load)
    for copy in inputs:
        copy.wait()

    of_owner = 7
    for distance in (1, -1):
        of_owner = of_owner + jnp.where(near(distance), 8, 0)
        of_owner = of_owner + jnp.where(far(distance), OWN, 0)
    two_steps = jnp.where((time == LAST - 1) | (time == NEXT + 1), OWN, 0)
    of_other = OWN * number((1, 0, -1))
    of_sender = of_other + number((1, -1)) + 1
    peers = jnp.where(is_owner, of_owner, jnp.where(on_core, of_sender, of_other))
    pl.semaphore_wait(barrier, peers + two_steps)

    def dual_copies(distance):
        slot = 1 - distance

        def copy(target, number):
            return pltpu.make_async_remote_copy(
                src_ref=y_ref,
                dst_ref=window_y.at[:, slot],
                send_sem=dual_sems.at[slot // 2 * 4 + number],
                recv_sem=halo_sems.at[slot],
                device_id=(2 * target + 1, at(distance)),
                device_id_type=MESH,
            )

        return [
            (on_core & far(distance) & at_end, [copy(left, 0), copy(left + 1, 1)]),
            (on_core & near(distance), [copy(place, 2)]),
        ]

    def pass_on(distance):
        slot = 1 + distance
        return pltpu.make_async_remote_copy(
            src_ref=window_y.at[:, slot],
            dst_ref=window_y.at[:, slot],
            send_sem=dual_sems.at[slot // 2 * 4 + 3],
            recv_sem=halo_sems.at[slot],
            device_id=(group - 1, time),
            device_id_type=MESH,
        )

    def rhs_copy(distance):
        slot = 1 - distance
        return pltpu.make_async_remote_copy(
            src_ref=rhs_ref.at[mine],
            dst_ref=window_rhs.at[slot],
            send_sem=halo_sems.at[slot + 4],
            recv_sem=halo_sems.at[slot + 1],
            device_id=(group, at(distance)),
            device_id_type=MESH,
        )

    for distance in (1, -1):
        for when, copies in dual_copies(distance):

            @pl.when(when)
            def _():
                for copy in copies:
                    copy.start()

    @pl.when(is_owner)
    def _():
        for distance in (1, -1):

            @pl.when(far(distance))
            def _():
                rhs_copy(distance).start()

    window_y[:, 1] = y_ref[...]
    window_rhs[1] = rhs_ref[mine]

    for chunk in range(NT // CHUNK):
        loads[chunk].wait()

        def turn(slot, carry):
            turned[slot] = staged[slot].T
            return carry

        if chunk * CHUNK < NT - FM:
            lax.fori_loop(chunk * CHUNK, (chunk + 1) * CHUNK, turn, 0, unroll=4)

        def halve(slot, carry):
            high, low = split(staged[slot])
            base = pl.multiple_of((slot - (NT - HALVED)) * TILE, TILE)
            weights[pl.ds(base, TILE), 0:TILE] = high
            weights[pl.ds(base, TILE), TILE : 2 * TILE] = low
            return carry

        if chunk * CHUNK >= NT - HALVED:
            lax.fori_loop(chunk * CHUNK, (chunk + 1) * CHUNK, halve, 0, unroll=4)

    var_class = class_ref[...]
    lower = jnp.zeros((CB, TILE), F32)
    upper = jnp.zeros((CB, TILE), F32)
    for class_id in range(lower_ref.shape[1]):
        lower = jnp.where(var_class == class_id, lower_ref[:, class_id : class_id + 1], lower)
        upper = jnp.where(var_class == class_id, upper_ref[:, class_id : class_id + 1], upper)

    first_row = (time - 1) * RB
    first_col = (group * 32 + time) * CB
    slot_id = lax.broadcasted_iota(jnp.int32, (WIN, NT), 1)
    window_id = lax.broadcasted_iota(jnp.int32, (WIN, NT), 0)
    owner_id = window_id // (3 * PIECE)
    block_id = window_id // PIECE - 3 * owner_id
    row_id = block_id * RB + owner_id * PIECE + lax.rem(window_id, PIECE)
    scatter = ((rowv_ref[...] - first_row) == row_id) & (slot_id < count_ref[0])
    gather = ((colv_ref[...] - first_col) == window_id[:CB]) & (slot_id[:CB] < count_ref[0])
    scatter = jnp.where(scatter, 1.0, 0.0)
    chosen = jnp.concatenate([scatter, jnp.where(gather, 1.0, 0.0)], axis=0)
    pick[...] = jnp.concatenate([scatter, scatter], axis=0).astype(BF16)
    if AM:
        last = scatter.T[NT - AM :]
        pick_last[...] = jnp.concatenate([last, last], axis=1).astype(BF16)
    chosen = chosen.astype(BF16)

    def spread(alone):
        width = 8 * (NT - alone) + alone
        lane = lax.broadcasted_iota(jnp.int32, (NT, width), 1)
        owner_slot = jnp.where(lane < 8 * (NT - alone), lane // 8, lane - 7 * (NT - alone))
        hit = owner_slot == lax.broadcasted_iota(jnp.int32, (NT, width), 0)
        return jnp.where(hit, 1.0, 0.0).astype(BF16)

    def twice(value):
        value = value.astype(BF16)
        return jnp.concatenate([value, value], axis=1)

    select_f[...] = twice(jnp.dot(chosen[:WIN], spread(FM), preferred_element_type=F32))
    select_a[...] = twice(
        jnp.dot(chosen[WIN:], spread(0)[:, : 8 * (NT - AM)], preferred_element_type=F32)
    )

    def add_up(select, values):
        high, low = split(values)
        return jnp.dot(select, jnp.concatenate([high, low], axis=0), preferred_element_type=F32)

    def fold(value):
        return jnp.sum(value.reshape(TILE // 8, 8, TILE), axis=0)

    sub_id = lax.broadcasted_iota(jnp.int32, (CB, TILE), 0)

    def adjoint(field):
        field = field[...].reshape(WIN, TILE)
        high, low = split(field.T)
        columns = jnp.dot(
            jnp.concatenate([high, low], axis=1), pick[...], preferred_element_type=F32
        )
        if AM:
            high, low = split(field)
            rows = lax.dot_general(
                pick_last[...],
                jnp.concatenate([high, low], axis=0),
                (((1,), (0,)), ((), ())),
                preferred_element_type=F32,
            )
            for index in range(AM):
                here = sub_id == cols_ref[NT - AM + index] - first_col
                value = rows[index : index + 1]
                high = value.astype(BF16).astype(F32)
                span = slice(index * TILE, (index + 1) * TILE)
                placed[0:CB, span] = jnp.where(here, high, 0.0).astype(BF16)
                placed[CB : 2 * CB, span] = jnp.where(here, value - high, 0.0).astype(BF16)
            total = jnp.dot(placed[...], weights[(HALVED - AM) * TILE :], preferred_element_type=F32)
            total = total[:CB] + total[CB:]
            total = total[:, :TILE] + total[:, TILE:]
        for slot in range(NT - AM):
            factor = jnp.broadcast_to(columns[:, slot : slot + 1], (TILE, TILE))
            partial[8 * slot : 8 * slot + 8] = fold(staged[slot] * factor)
        rest = add_up(select_a[...], partial[0 : 8 * (NT - AM)])
        return total + rest if AM else rest

    def forward(field):
        if FM:
            high, low = split(field)
            halves = jnp.concatenate([high, low], axis=0)
            result = lax.dot_general(
                jnp.concatenate([halves, halves], axis=1),
                weights[(HALVED - FM) * TILE :],
                (((1,), (1,)), ((), ())),
                preferred_element_type=F32,
            )
            for index in range(FM):
                span = slice(index * TILE, (index + 1) * TILE)
                product[index] = result[:CB, span] + result[CB:, span]
        columns = field.T
        for block in range(CB):
            factors[block] = jnp.broadcast_to(columns[:, block : block + 1], (TILE, TILE))

        def product_of(slot, carry):
            col = jnp.clip(cols_ref[slot] - first_col, 0, CB - 1)
            partial[pl.ds(pl.multiple_of(8 * slot, 8), 8)] = fold(turned[slot] * factors[col])
            return carry

        lax.fori_loop(0, NT - FM, product_of, 0, unroll=16)
        for index in range(FM):
            col = jnp.clip(cols_ref[NT - FM + index] - first_col, 0, CB - 1)
            row = 8 * (NT - FM) + index
            partial[row : row + 1] = product[index, pl.ds(col, 1), :]
        return add_up(select_f[...], partial[0 : 8 * (NT - FM) + FM])

    def primal_update(primal, adjoint_part):
        moved = primal - STEP * (cost_ref[...] - adjoint_part)
        return jnp.minimum(jnp.maximum(moved, lower), upper)

    def to_owner(source, target, distance, offset, sems):
        return pltpu.make_async_remote_copy(
            src_ref=source,
            dst_ref=target,
            send_sem=sums_sent.at[sems, distance + 2],
            recv_sem=sums_recv.at[sems, 2 - distance],
            device_id=(owner_group(offset), at(distance)),
            device_id_type=MESH,
        )

    def from_owner(source, target, offset, distance, semaphore):
        return pltpu.make_async_remote_copy(
            src_ref=source,
            dst_ref=target,
            send_sem=send_sems.at[semaphore],
            recv_sem=recv_sems.at[semaphore],
            device_id=(lax.rem(group + offset, 8), at(distance)),
            device_id_type=MESH,
        )

    def rows_of(ref, first, pieces):
        return ref.at[pl.ds(pl.multiple_of(first, PIECE), pieces * PIECE)]

    def copy_a(distance, offset, pieces):
        block = jnp.where(time == NEXT, 0, 1) if distance == 0 else 2 if distance > 0 else 0
        if pieces == 2:
            block = jnp.where(time == NEXT, 0, 1)
        region = {
            0: 0,
            1: jnp.where(time + 1 == NEXT, 2, 4),
            -1: jnp.where(time - 1 == NEXT, 4, 2),
            2: 5,
            -2: 5,
        }[distance]
        if distance == 0 and pieces == 1:
            block = 1
        source = rows_of(terms_a, (owner(offset) * 3 + block) * PIECE, pieces)
        target = rows_of(parts_a, group * SLOT_ROWS + region * PIECE, pieces)
        return to_owner(source, target, distance, offset, 0)

    def copy_b(distance, offset):
        source = rows_of(terms_b, (owner(offset) * 3 + 1 + distance) * PIECE, 1)
        target = rows_of(parts_b, (group * 3 + 1 - distance) * PIECE, 1)
        return to_owner(source, target, distance, offset, 1)

    def to_owners(distance, copy):
        for offset in (1, 0):
            if distance or offset:
                copy(distance, offset).start()
            else:

                @pl.when(jnp.logical_not(is_owner))
                def _():
                    copy(distance, offset).start()

    def steps_a():
        for distance in (1, -1, 0):
            yield distance, exists(distance) & both(distance), 2
        for distance in (1, -1, 0):
            yield distance, exists(distance) & jnp.logical_not(both(distance)), 1

    def wait_rows(semaphore, pieces):
        ref = parts_a.at[0 : pieces * PIECE]
        pltpu.make_async_copy(ref, ref, semaphore).wait()

    def wait_sums_a(semaphores, two_steps, copies, own):
        for distance, when, pieces in steps_a():

            @pl.when(when)
            def _():
                wait_rows(semaphores.at[0, distance + 2], pieces * (copies if distance else own))

        for distance, when in two_steps:

            @pl.when(when)
            def _():
                wait_rows(semaphores.at[0, distance + 2], copies)

    def wait_sums_b(semaphores, copies, own):
        for distance in (1, -1, 0):

            @pl.when(exists(distance))
            def _():
                wait_rows(semaphores.at[1, distance + 2], copies if distance else own)

    for distance, when in ((1, near(1)), (-1, near(-1)), (1, far(1)), (-1, far(-1))):

        @pl.when(when)
        def _():
            dual_in = window_y.at[:, 1 + distance]
            pltpu.make_async_copy(dual_in, dual_in, halo_sems.at[1 + distance]).wait()

            @pl.when(on_core)
            def _():
                pass_on(distance).start()

    primal_0 = x_ref[...]
    primal_1 = primal_update(primal_0, adjoint(window_y))
    terms_a[...] = forward(2.0 * primal_1 - primal_0)
    for distance, when in ((2, time == LAST - 1), (-2, time == NEXT + 1)):

        @pl.when(when)
        def _():
            to_owners(distance, lambda distance, offset: copy_a(distance, offset, 1))

    for distance, when, pieces in steps_a():

        @pl.when(when)
        def _():
            to_owners(distance, lambda distance, offset: copy_a(distance, offset, pieces))

    @pl.when(is_owner)
    def _():
        for pieces, when in ((2, edge), (1, jnp.logical_not(edge))):

            @pl.when(when)
            def _():
                block = jnp.where(time == NEXT, 0, 1) if pieces == 2 else 1
                source = pl.ds(pl.multiple_of((mine * 3 + block) * PIECE, 8), pieces * PIECE)
                target = pl.ds(pl.multiple_of(group * SLOT_ROWS, 8), pieces * PIECE)
                parts_a[target] = terms_a[source]

        def summed(ref, stride, first):
            return sum(
                ref[pl.ds(pl.multiple_of((index * stride + first) * PIECE, PIECE), PIECE)] for index in range(8)
            )

        for distance, when, pieces in steps_a():

            @pl.when(when & jnp.logical_not(far(distance) if distance else False))
            def _():
                wait_rows(sums_recv.at[0, distance + 2], pieces * (8 if distance else 7))

        early = [summed(parts_a, 6, index) for index in (0, 1, 4)]
        for distance in (1, -1):

            @pl.when(far(distance))
            def _():
                rhs_in = window_rhs.at[1 + distance]
                pltpu.make_async_copy(rhs_in, rhs_in, halo_sems.at[2 + distance]).wait()
                wait_rows(sums_recv.at[0, distance + 2], 2 * 8)

        for distance, when in ((2, time == LAST), (-2, time == NEXT)):

            @pl.when(when)
            def _():
                wait_rows(sums_recv.at[0, distance + 2], 8)

        step = [early[0], early[1], summed(parts_a, 6, 2), summed(parts_a, 6, 3), early[2], summed(parts_a, 6, 5)]
        low = step[0] + step[2]
        high = step[1] + step[3]
        upper_side = time == NEXT
        first = jnp.where(upper_side, high, low) + step[4]
        second = jnp.where(upper_side, low, high) + step[5]
        for block in range(3):
            image = first if block == 1 else second
            piece_a[block] = jnp.maximum(window_y[mine, block] + STEP * (window_rhs[block] - image), 0.0)
        @pl.when(edge)
        def _():
            span = pl.ds(jnp.where(time == NEXT, 0, 1), 2)
            for offset in (3, 5, 1, 7, 4, 2, 6):
                from_owner(piece_a.at[span], window_next.at[mine, span], offset, 0, 0).start()
            window_next[mine, span] = piece_a[span]

        @pl.when(jnp.logical_not(edge))
        def _():
            for offset in (3, 5, 1, 7, 4, 2, 6):
                from_owner(piece_a.at[1], window_next.at[mine, 1], offset, 0, 0).start()
            window_next[mine, 1] = piece_a[1]

        for distance in (1, -1):

            @pl.when(near(distance))
            def _():
                for offset in range(7, -1, -1):
                    from_owner(
                        piece_a.at[1], window_next.at[mine, 1 - distance], offset, distance, 2 + distance
                    ).start()

    for owned, others in ((is_owner, OWN - 1), (jnp.logical_not(is_owner), OWN)):
        for pieces, when in ((2, edge), (1, jnp.logical_not(edge))):

            @pl.when(owned & when)
            def _():
                wait_rows(recv_sems.at[0], pieces * others)

    for distance in (1, -1):

        @pl.when(near(distance))
        def _():
            wait_rows(recv_sems.at[2 - distance], OWN)

    primal_2 = primal_update(primal_1, adjoint(window_next))
    terms_b[...] = forward(2.0 * primal_2 - primal_1)
    for distance in (1, -1, 0):

        @pl.when(exists(distance))
        def _():
            to_owners(distance, copy_b)

    primals[0] = primal_1
    primals[1] = primal_2
    results = [
        pltpu.make_async_copy(primals, primal_out, out_sems.at[0]),
        pltpu.make_async_copy(window_next.at[:, 1], dual_out.at[0], out_sems.at[1]),
    ]
    for copy in results:
        copy.start()


    @pl.when(is_owner)
    def _():
        own = pl.ds(pl.multiple_of(mine * 3 * PIECE + PIECE, 8), PIECE)
        parts_b[pl.ds(pl.multiple_of(group * 3 * PIECE + PIECE, 8), PIECE)] = terms_b[own]
        def summed(first):
            return sum(
                parts_b[pl.ds(pl.multiple_of((index * 3 + first) * PIECE, PIECE), PIECE)] for index in range(8)
            )

        wait_rows(sums_recv.at[1, 2], 7)
        for distance in (1, -1):

            @pl.when(near(distance))
            def _():
                wait_rows(sums_recv.at[1, distance + 2], 8)

        near_block = jnp.where(time == LAST, 0, 2)
        early = summed(1) + summed(near_block)
        for distance in (1, -1):

            @pl.when(far(distance))
            def _():
                wait_rows(sums_recv.at[1, distance + 2], 8)

        image = early + summed(2 - near_block)
        piece_b[...] = jnp.maximum(piece_a[1] + STEP * (window_rhs[1] - image), 0.0)
        for offset in (3, 5, 1, 7, 4, 2, 6):
            from_owner(piece_b, dual_out.at[1, mine], offset, 0, 2).start()
        own_copy = pltpu.make_async_copy(piece_b, dual_out.at[1, mine], out_sems.at[2])
        own_copy.start()
        wait_rows(recv_sems.at[2], OWN - 1)
        own_copy.wait()

    @pl.when(jnp.logical_not(is_owner))
    def _():
        wait_rows(recv_sems.at[2], OWN)

    for copy in results:
        copy.wait()

    for distance in (1, -1):
        for when, copies in dual_copies(distance):

            @pl.when(when)
            def _():
                for copy in copies:
                    copy.wait_send()

    for distance in (1, -1):

        @pl.when(on_core & exists(distance))
        def _():
            pass_on(distance).wait_send()

    two_steps = ((2, time == LAST - 1), (-2, time == NEXT + 1))

    @pl.when(is_owner)
    def _():
        for distance in (1, -1):

            @pl.when(far(distance))
            def _():
                rhs_copy(distance).wait_send()

            @pl.when(near(distance))
            def _():
                wait_rows(send_sems.at[2 + distance], 8)

        wait_sums_a(sums_sent, two_steps, OWN, OWN - 1)
        wait_sums_b(sums_sent, OWN, OWN - 1)
        for pieces, when in ((2, edge), (1, jnp.logical_not(edge))):

            @pl.when(when)
            def _():
                wait_rows(send_sems.at[0], 7 * pieces)

        wait_rows(send_sems.at[2], 7)

    @pl.when(jnp.logical_not(is_owner))
    def _():
        wait_sums_a(sums_sent, two_steps, OWN, OWN)
        wait_sums_b(sums_sent, OWN, OWN)


def means(primals_ref, duals_ref, primal_out, dual_out, primal_mean_out, dual_mean_out):
    for iterates, last, mean in ((primals_ref, primal_out, primal_mean_out), (duals_ref, dual_out, dual_mean_out)):
        last[...] = iterates[1]
        mean[...] = (iterates[0] + iterates[1]) / ITERS


def body(
    x_start,
    y_start,
    cost,
    rhs,
    tiles,
    tile_rows,
    tile_cols,
    tile_count,
    var_class,
    lower_table,
    upper_table,
):
    vmem = pl.BlockSpec(memory_space=pltpu.VMEM)
    primals, duals = pl.pallas_call(
        kernel,
        name="pdhg",
        out_shape=(
            jax.ShapeDtypeStruct((ITERS, CB, TILE), F32),
            jax.ShapeDtypeStruct((ITERS, OWN, PIECE, TILE), F32),
        ),
        in_specs=[pl.BlockSpec(memory_space=pltpu.HBM)] * 12,
        out_specs=(pl.BlockSpec(memory_space=pl.ANY),) * 2,
        scratch_shapes=[
            pltpu.VMEM((CB, TILE), F32),
            pltpu.VMEM((OWN, PIECE, TILE), F32),
            pltpu.VMEM((CB, TILE), F32),
            pltpu.VMEM((OWN, PIECE, TILE), F32),
            pltpu.SMEM((NT,), jnp.int32),
            pltpu.SMEM((1,), jnp.int32),
            pltpu.VMEM((1, NT), jnp.int32),
            pltpu.VMEM((1, NT), jnp.int32),
            pltpu.VMEM((CB, TILE), jnp.int32),
            pltpu.VMEM((1, 8), F32),
            pltpu.VMEM((1, 8), F32),
            pltpu.VMEM((NT, TILE, TILE), F32),
            pltpu.VMEM((NT, TILE, TILE), F32),
            pltpu.VMEM((CB, TILE, TILE), F32),
            pltpu.VMEM((max(HALVED, 1) * TILE, 2 * TILE), BF16),
            pltpu.VMEM((2 * CB, max(AM, 1) * TILE), BF16),
            pltpu.VMEM((max(FM, 1), CB, TILE), F32),
            pltpu.VMEM((WIN, 16 * (NT - FM) + 2 * FM), BF16),
            pltpu.VMEM((CB, 16 * (NT - AM)), BF16),
            pltpu.VMEM((8 * NT, TILE), F32),
            pltpu.VMEM((2 * WIN, NT), BF16),
            pltpu.VMEM((max(AM, 1), 2 * WIN), BF16),
            pltpu.VMEM((OWN, 3, PIECE, TILE), F32),
            pltpu.VMEM((3, PIECE, TILE), F32),
            pltpu.VMEM((OWN, 3, PIECE, TILE), F32),
            pltpu.VMEM((WIN, TILE), F32),
            pltpu.VMEM((WIN, TILE), F32),
            pltpu.VMEM((8 * SLOT_ROWS, TILE), F32),
            pltpu.VMEM((8 * 3 * PIECE, TILE), F32),
            pltpu.VMEM((3, PIECE, TILE), F32),
            pltpu.VMEM((PIECE, TILE), F32),
            pltpu.VMEM((ITERS, CB, TILE), F32),
            pltpu.SemaphoreType.DMA((NT // CHUNK,)),
            pltpu.SemaphoreType.DMA((3,)),
            pltpu.SemaphoreType.DMA((11,)),
            pltpu.SemaphoreType.DMA((8,)),
            pltpu.SemaphoreType.DMA((8,)),
            pltpu.SemaphoreType.DMA((2, 5)),
            pltpu.SemaphoreType.DMA((2, 5)),
            pltpu.SemaphoreType.DMA((4,)),
            pltpu.SemaphoreType.DMA((4,)),
        ],
        compiler_params=pltpu.CompilerParams(
            collective_id=0, has_side_effects=True, vmem_limit_bytes=60 * 1024 * 1024
        ),
    )(
        x_start,
        y_start.reshape(OWN, PIECE, TILE),
        cost,
        rhs.reshape(OWN, PIECE, TILE),
        tiles,
        tile_cols,
        tile_count,
        tile_rows.reshape(1, NT),
        tile_cols.reshape(1, NT),
        var_class,
        lower_table.reshape(1, 8),
        upper_table.reshape(1, 8),
    )
    columns = jax.ShapeDtypeStruct((CB, TILE), F32)
    rows = jax.ShapeDtypeStruct((RB, TILE), F32)
    return pl.pallas_call(
        means,
        name="means",
        out_shape=(columns, rows, columns, rows),
        in_specs=[vmem, vmem],
        out_specs=(vmem, vmem, vmem, vmem),
    )(primals, duals.reshape(ITERS, RB, TILE))


def solution(mesh):
    return jax.shard_map(
        body,
        mesh=mesh,
        in_specs=(
            P(("grp", "tm"), None),
            P("tm", None),
            P(("grp", "tm"), None),
            P("tm", None),
            P(("grp", "tm"), None, None),
            P(("grp", "tm")),
            P(("grp", "tm")),
            P(("grp", "tm")),
            P(("grp", "tm"), None),
            P(),
            P(),
        ),
        out_specs=(P(("grp", "tm"), None), P("tm", None), P(("grp", "tm"), None), P("tm", None)),
        check_vma=False,
    )
```

```python
import jax
import jax.numpy as jnp
from jax import lax
from jax.experimental import pallas as pl
from jax.experimental.pallas import tpu as pltpu
from jax.sharding import PartitionSpec as P

ITERS = 2
STEP = 0.6
MESH = pl.DeviceIdType.MESH
F32 = jnp.float32
BF16 = jnp.bfloat16

NT = 64
TILE = 128
CB = 16
RB = 32
OWN = 2
PIECE = RB // OWN
WIN = 3 * RB
CHUNK = 8
AM = 40
FM = 16
HALVED = max(AM, FM)

LAST, NEXT = 15, 16
SLOT_ROWS = 6 * PIECE


def split(value):
    high = value.astype(BF16)
    return high, (value - high.astype(F32)).astype(BF16)


def kernel(
    x_hbm,
    y_hbm,
    cost_hbm,
    rhs_hbm,
    tiles_hbm,
    cols_hbm,
    count_hbm,
    rowv_hbm,
    colv_hbm,
    class_hbm,
    lower_hbm,
    upper_hbm,
    primal_out,
    dual_out,
    x_ref,
    y_ref,
    cost_ref,
    rhs_ref,
    cols_ref,
    count_ref,
    rowv_ref,
    colv_ref,
    class_ref,
    lower_ref,
    upper_ref,
    staged,
    turned,
    factors,
    weights,
    placed,
    product,
    select_f,
    select_a,
    partial,
    pick,
    pick_last,
    window_y,
    window_rhs,
    window_next,
    terms_a,
    terms_b,
    parts_a,
    parts_b,
    piece_a,
    piece_b,
    primals,
    load_sem,
    out_sems,
    input_sems,
    dual_sems,
    halo_sems,
    sums_sent,
    sums_recv,
    send_sems,
    recv_sems,
):
    group = lax.axis_index("grp")
    time = lax.axis_index("tm")
    place = group // 2
    core = lax.rem(group, 2)
    on_core = core == 1
    is_owner = on_core & ((place == 1) | (place == 2))
    mine = place // 2

    def at(distance):
        return time + distance

    def exists(distance):
        there = time + distance
        return (there >= 0) & (there < 32)

    def number(distances):
        return sum(jnp.where(exists(distance), 1, 0) for distance in distances)

    def owner(offset):
        return lax.rem(mine + offset, OWN)

    def owner_group(offset):
        return 2 * owner(offset) + 3

    def far(distance):
        return (time == LAST) if distance > 0 else (time == NEXT)

    def near(distance):
        return exists(distance) & jnp.logical_not(far(distance))

    edge = (time == LAST) | (time == NEXT)
    at_end = (place == 0) | (place == 3)

    def both(distance):
        return edge if distance == 0 else far(distance)

    window_rhs[...] = jnp.zeros_like(window_rhs)

    @pl.when(jnp.logical_not(edge))
    def _():
        parts_a[...] = jnp.zeros_like(parts_a)

    @pl.when((time == 0) | (time == 31))
    def _():
        parts_b[...] = jnp.zeros_like(parts_b)
        window_y[...] = jnp.zeros_like(window_y)
        window_next[...] = jnp.zeros_like(window_next)

    barrier = pltpu.get_barrier_semaphore()

    def greet(target_group, target_time):
        pl.semaphore_signal(
            barrier, inc=1, device_id=(target_group, target_time), device_id_type=MESH
        )

    def greet_all(distance):
        for offset in range(7, -1, -1):
            if distance or offset:
                greet(lax.rem(group + offset, 8), at(distance))

    source_place = jnp.where(place >= 2, 0, 3)
    left = jnp.where(place == 3, 0, 2)

    @pl.when(is_owner)
    def _():
        for distance, when in ((2, time == LAST), (-2, time == NEXT), (1, exists(1)), (-1, exists(-1))):

            @pl.when(when)
            def _():
                greet_all(distance)

        greet_all(0)

    @pl.when(jnp.logical_not(is_owner))
    def _():
        for distance in (1, -1):

            @pl.when(on_core & far(distance))
            def _():
                greet(2 * source_place + 1, at(distance))

            @pl.when(on_core & near(distance))
            def _():
                greet(group, at(distance))

            @pl.when(near(distance))
            def _():
                for offset in range(OWN):
                    greet(owner_group(offset), at(distance))

        for offset in range(OWN):
            greet(owner_group(offset), time)

        @pl.when(jnp.logical_not(on_core) & at_end)
        def _():
            greet(group + 1, time)

    inputs = []
    for index, (source, target) in enumerate(
        (
            (y_hbm, y_ref),
            (rhs_hbm, rhs_ref),
            (x_hbm, x_ref),
            (cost_hbm, cost_ref),
            (class_hbm, class_ref),
            (rowv_hbm, rowv_ref),
            (colv_hbm, colv_ref),
            (count_hbm, count_ref),
            (lower_hbm, lower_ref),
            (upper_hbm, upper_ref),
            (cols_hbm, cols_ref),
        )
    ):
        copy = pltpu.make_async_copy(source, target, input_sems.at[index])
        copy.start()
        inputs.append(copy)
    loads = []
    for chunk in range(NT // CHUNK):
        span = pl.ds(chunk * CHUNK, CHUNK)
        load = pltpu.make_async_copy(tiles_hbm.at[span], staged.at[span], load_sem.at[chunk])
        load.start()
        loads.append(load)
    for copy in inputs:
        copy.wait()

    of_owner = 7
    for distance in (1, -1):
        of_owner = of_owner + jnp.where(near(distance), 8, 0)
        of_owner = of_owner + jnp.where(far(distance), OWN, 0)
    two_steps = jnp.where((time == LAST - 1) | (time == NEXT + 1), OWN, 0)
    of_other = OWN * number((1, 0, -1))
    of_sender = of_other + number((1, -1)) + 1
    peers = jnp.where(is_owner, of_owner, jnp.where(on_core, of_sender, of_other))
    pl.semaphore_wait(barrier, peers + two_steps)

    def dual_copies(distance):
        slot = 1 - distance

        def copy(target, number):
            return pltpu.make_async_remote_copy(
                src_ref=y_ref,
                dst_ref=window_y.at[:, slot],
                send_sem=dual_sems.at[slot // 2 * 4 + number],
                recv_sem=halo_sems.at[slot],
                device_id=(2 * target + 1, at(distance)),
                device_id_type=MESH,
            )

        return [
            (on_core & far(distance) & at_end, [copy(left, 0), copy(left + 1, 1)]),
            (on_core & near(distance), [copy(place, 2)]),
        ]

    def pass_on(distance):
        slot = 1 + distance
        return pltpu.make_async_remote_copy(
            src_ref=window_y.at[:, slot],
            dst_ref=window_y.at[:, slot],
            send_sem=dual_sems.at[slot // 2 * 4 + 3],
            recv_sem=halo_sems.at[slot],
            device_id=(group - 1, time),
            device_id_type=MESH,
        )

    def rhs_copy(distance):
        slot = 1 - distance
        return pltpu.make_async_remote_copy(
            src_ref=rhs_ref.at[mine],
            dst_ref=window_rhs.at[slot],
            send_sem=halo_sems.at[slot + 4],
            recv_sem=halo_sems.at[slot + 1],
            device_id=(group, at(distance)),
            device_id_type=MESH,
        )

    for distance in (1, -1):
        for when, copies in dual_copies(distance):

            @pl.when(when)
            def _():
                for copy in copies:
                    copy.start()

    @pl.when(is_owner)
    def _():
        for distance in (1, -1):

            @pl.when(far(distance))
            def _():
                rhs_copy(distance).start()

    window_y[:, 1] = y_ref[...]
    window_rhs[1] = rhs_ref[mine]

    for chunk in range(NT // CHUNK):
        loads[chunk].wait()

        def turn(slot, carry):
            turned[slot] = staged[slot].T
            return carry

        if chunk * CHUNK < NT - FM:
            lax.fori_loop(chunk * CHUNK, (chunk + 1) * CHUNK, turn, 0, unroll=4)

        def halve(slot, carry):
            high, low = split(staged[slot])
            base = pl.multiple_of((slot - (NT - HALVED)) * TILE, TILE)
            weights[pl.ds(base, TILE), 0:TILE] = high
            weights[pl.ds(base, TILE), TILE : 2 * TILE] = low
            return carry

        if chunk * CHUNK >= NT - HALVED:
            lax.fori_loop(chunk * CHUNK, (chunk + 1) * CHUNK, halve, 0, unroll=4)

    var_class = class_ref[...]
    lower = jnp.zeros((CB, TILE), F32)
    upper = jnp.zeros((CB, TILE), F32)
    for class_id in range(lower_ref.shape[1]):
        lower = jnp.where(var_class == class_id, lower_ref[:, class_id : class_id + 1], lower)
        upper = jnp.where(var_class == class_id, upper_ref[:, class_id : class_id + 1], upper)

    first_row = (time - 1) * RB
    first_col = (group * 32 + time) * CB
    slot_id = lax.broadcasted_iota(jnp.int32, (WIN, NT), 1)
    window_id = lax.broadcasted_iota(jnp.int32, (WIN, NT), 0)
    owner_id = window_id // (3 * PIECE)
    block_id = window_id // PIECE - 3 * owner_id
    row_id = block_id * RB + owner_id * PIECE + lax.rem(window_id, PIECE)
    scatter = ((rowv_ref[...] - first_row) == row_id) & (slot_id < count_ref[0])
    gather = ((colv_ref[...] - first_col) == window_id[:CB]) & (slot_id[:CB] < count_ref[0])
    scatter = jnp.where(scatter, 1.0, 0.0)
    chosen = jnp.concatenate([scatter, jnp.where(gather, 1.0, 0.0)], axis=0)
    pick[...] = jnp.concatenate([scatter, scatter], axis=0).astype(BF16)
    if AM:
        last = scatter.T[NT - AM :]
        pick_last[...] = jnp.concatenate([last, last], axis=1).astype(BF16)
    chosen = chosen.astype(BF16)

    def spread(alone):
        width = 8 * (NT - alone) + alone
        lane = lax.broadcasted_iota(jnp.int32, (NT, width), 1)
        owner_slot = jnp.where(lane < 8 * (NT - alone), lane // 8, lane - 7 * (NT - alone))
        hit = owner_slot == lax.broadcasted_iota(jnp.int32, (NT, width), 0)
        return jnp.where(hit, 1.0, 0.0).astype(BF16)

    def twice(value):
        value = value.astype(BF16)
        return jnp.concatenate([value, value], axis=1)

    select_f[...] = twice(jnp.dot(chosen[:WIN], spread(FM), preferred_element_type=F32))
    select_a[...] = twice(
        jnp.dot(chosen[WIN:], spread(0)[:, : 8 * (NT - AM)], preferred_element_type=F32)
    )

    def add_up(select, values):
        high, low = split(values)
        return jnp.dot(select, jnp.concatenate([high, low], axis=0), preferred_element_type=F32)

    def fold(value):
        return jnp.sum(value.reshape(TILE // 8, 8, TILE), axis=0)

    sub_id = lax.broadcasted_iota(jnp.int32, (CB, TILE), 0)

    def adjoint(field):
        field = field[...].reshape(WIN, TILE)
        high, low = split(field.T)
        columns = jnp.dot(
            jnp.concatenate([high, low], axis=1), pick[...], preferred_element_type=F32
        )
        if AM:
            high, low = split(field)
            rows = lax.dot_general(
                pick_last[...],
                jnp.concatenate([high, low], axis=0),
                (((1,), (0,)), ((), ())),
                preferred_element_type=F32,
            )
            for index in range(AM):
                here = sub_id == cols_ref[NT - AM + index] - first_col
                value = rows[index : index + 1]
                high = value.astype(BF16).astype(F32)
                span = slice(index * TILE, (index + 1) * TILE)
                placed[0:CB, span] = jnp.where(here, high, 0.0).astype(BF16)
                placed[CB : 2 * CB, span] = jnp.where(here, value - high, 0.0).astype(BF16)
            total = jnp.dot(placed[...], weights[(HALVED - AM) * TILE :], preferred_element_type=F32)
            total = total[:CB] + total[CB:]
            total = total[:, :TILE] + total[:, TILE:]
        for slot in range(NT - AM):
            factor = jnp.broadcast_to(columns[:, slot : slot + 1], (TILE, TILE))
            partial[8 * slot : 8 * slot + 8] = fold(staged[slot] * factor)
        rest = add_up(select_a[...], partial[0 : 8 * (NT - AM)])
        return total + rest if AM else rest

    def forward(field):
        if FM:
            high, low = split(field)
            halves = jnp.concatenate([high, low], axis=0)
            result = lax.dot_general(
                jnp.concatenate([halves, halves], axis=1),
                weights[(HALVED - FM) * TILE :],
                (((1,), (1,)), ((), ())),
                preferred_element_type=F32,
            )
            for index in range(FM):
                span = slice(index * TILE, (index + 1) * TILE)
                product[index] = result[:CB, span] + result[CB:, span]
        columns = field.T
        for block in range(CB):
            factors[block] = jnp.broadcast_to(columns[:, block : block + 1], (TILE, TILE))

        def product_of(slot, carry):
            col = jnp.clip(cols_ref[slot] - first_col, 0, CB - 1)
            partial[pl.ds(pl.multiple_of(8 * slot, 8), 8)] = fold(turned[slot] * factors[col])
            return carry

        lax.fori_loop(0, NT - FM, product_of, 0, unroll=16)
        for index in range(FM):
            col = jnp.clip(cols_ref[NT - FM + index] - first_col, 0, CB - 1)
            row = 8 * (NT - FM) + index
            partial[row : row + 1] = product[index, pl.ds(col, 1), :]
        return add_up(select_f[...], partial[0 : 8 * (NT - FM) + FM])

    def primal_update(primal, adjoint_part):
        moved = primal - STEP * (cost_ref[...] - adjoint_part)
        return jnp.minimum(jnp.maximum(moved, lower), upper)

    def to_owner(source, target, distance, offset, sems):
        return pltpu.make_async_remote_copy(
            src_ref=source,
            dst_ref=target,
            send_sem=sums_sent.at[sems, distance + 2],
            recv_sem=sums_recv.at[sems, 2 - distance],
            device_id=(owner_group(offset), at(distance)),
            device_id_type=MESH,
        )

    def from_owner(source, target, offset, distance, semaphore):
        return pltpu.make_async_remote_copy(
            src_ref=source,
            dst_ref=target,
            send_sem=send_sems.at[semaphore],
            recv_sem=recv_sems.at[semaphore],
            device_id=(lax.rem(group + offset, 8), at(distance)),
            device_id_type=MESH,
        )

    def rows_of(ref, first, pieces):
        return ref.at[pl.ds(pl.multiple_of(first, PIECE), pieces * PIECE)]

    def copy_a(distance, offset, pieces):
        block = jnp.where(time == NEXT, 0, 1) if distance == 0 else 2 if distance > 0 else 0
        if pieces == 2:
            block = jnp.where(time == NEXT, 0, 1)
        region = {
            0: 0,
            1: jnp.where(time + 1 == NEXT, 2, 4),
            -1: jnp.where(time - 1 == NEXT, 4, 2),
            2: 5,
            -2: 5,
        }[distance]
        if distance == 0 and pieces == 1:
            block = 1
        source = rows_of(terms_a, (owner(offset) * 3 + block) * PIECE, pieces)
        target = rows_of(parts_a, group * SLOT_ROWS + region * PIECE, pieces)
        return to_owner(source, target, distance, offset, 0)

    def copy_b(distance, offset):
        source = rows_of(terms_b, (owner(offset) * 3 + 1 + distance) * PIECE, 1)
        target = rows_of(parts_b, (group * 3 + 1 - distance) * PIECE, 1)
        return to_owner(source, target, distance, offset, 1)

    def to_owners(distance, copy):
        for offset in (1, 0):
            if distance or offset:
                copy(distance, offset).start()
            else:

                @pl.when(jnp.logical_not(is_owner))
                def _():
                    copy(distance, offset).start()

    def steps_a():
        for distance in (1, -1, 0):
            yield distance, exists(distance) & both(distance), 2
        for distance in (1, -1, 0):
            yield distance, exists(distance) & jnp.logical_not(both(distance)), 1

    def wait_rows(semaphore, pieces):
        ref = parts_a.at[0 : pieces * PIECE]
        pltpu.make_async_copy(ref, ref, semaphore).wait()

    def wait_sums_a(semaphores, two_steps, copies, own):
        for distance, when, pieces in steps_a():

            @pl.when(when)
            def _():
                wait_rows(semaphores.at[0, distance + 2], pieces * (copies if distance else own))

        for distance, when in two_steps:

            @pl.when(when)
            def _():
                wait_rows(semaphores.at[0, distance + 2], copies)

    def wait_sums_b(semaphores, copies, own):
        for distance in (1, -1, 0):

            @pl.when(exists(distance))
            def _():
                wait_rows(semaphores.at[1, distance + 2], copies if distance else own)

    for distance, when in ((1, near(1)), (-1, near(-1)), (1, far(1)), (-1, far(-1))):

        @pl.when(when)
        def _():
            dual_in = window_y.at[:, 1 + distance]
            pltpu.make_async_copy(dual_in, dual_in, halo_sems.at[1 + distance]).wait()

            @pl.when(on_core)
            def _():
                pass_on(distance).start()

    primal_0 = x_ref[...]
    primal_1 = primal_update(primal_0, adjoint(window_y))
    terms_a[...] = forward(2.0 * primal_1 - primal_0)
    for distance, when in ((2, time == LAST - 1), (-2, time == NEXT + 1)):

        @pl.when(when)
        def _():
            to_owners(distance, lambda distance, offset: copy_a(distance, offset, 1))

    for distance, when, pieces in steps_a():

        @pl.when(when)
        def _():
            to_owners(distance, lambda distance, offset: copy_a(distance, offset, pieces))

    @pl.when(is_owner)
    def _():
        for pieces, when in ((2, edge), (1, jnp.logical_not(edge))):

            @pl.when(when)
            def _():
                block = jnp.where(time == NEXT, 0, 1) if pieces == 2 else 1
                source = pl.ds(pl.multiple_of((mine * 3 + block) * PIECE, 8), pieces * PIECE)
                target = pl.ds(pl.multiple_of(group * SLOT_ROWS, 8), pieces * PIECE)
                parts_a[target] = terms_a[source]

        def summed(ref, stride, first):
            return sum(
                ref[pl.ds(pl.multiple_of((index * stride + first) * PIECE, PIECE), PIECE)] for index in range(8)
            )

        for distance, when, pieces in steps_a():

            @pl.when(when & jnp.logical_not(far(distance) if distance else False))
            def _():
                wait_rows(sums_recv.at[0, distance + 2], pieces * (8 if distance else 7))

        early = [summed(parts_a, 6, index) for index in (0, 1, 4)]
        for distance in (1, -1):

            @pl.when(far(distance))
            def _():
                rhs_in = window_rhs.at[1 + distance]
                pltpu.make_async_copy(rhs_in, rhs_in, halo_sems.at[2 + distance]).wait()
                wait_rows(sums_recv.at[0, distance + 2], 2 * 8)

        for distance, when in ((2, time == LAST), (-2, time == NEXT)):

            @pl.when(when)
            def _():
                wait_rows(sums_recv.at[0, distance + 2], 8)

        step = [early[0], early[1], summed(parts_a, 6, 2), summed(parts_a, 6, 3), early[2], summed(parts_a, 6, 5)]
        low = step[0] + step[2]
        high = step[1] + step[3]
        upper_side = time == NEXT
        first = jnp.where(upper_side, high, low) + step[4]
        second = jnp.where(upper_side, low, high) + step[5]
        for block in range(3):
            image = first if block == 1 else second
            piece_a[block] = jnp.maximum(window_y[mine, block] + STEP * (window_rhs[block] - image), 0.0)
        @pl.when(edge)
        def _():
            span = pl.ds(jnp.where(time == NEXT, 0, 1), 2)
            for offset in (3, 5, 1, 7, 4, 2, 6):
                from_owner(piece_a.at[span], window_next.at[mine, span], offset, 0, 0).start()
            window_next[mine, span] = piece_a[span]

        @pl.when(jnp.logical_not(edge))
        def _():
            for offset in (3, 5, 1, 7, 4, 2, 6):
                from_owner(piece_a.at[1], window_next.at[mine, 1], offset, 0, 0).start()
            window_next[mine, 1] = piece_a[1]

        for distance in (1, -1):

            @pl.when(near(distance))
            def _():
                for offset in range(7, -1, -1):
                    from_owner(
                        piece_a.at[1], window_next.at[mine, 1 - distance], offset, distance, 2 + distance
                    ).start()

    for owned, others in ((is_owner, OWN - 1), (jnp.logical_not(is_owner), OWN)):
        for pieces, when in ((2, edge), (1, jnp.logical_not(edge))):

            @pl.when(owned & when)
            def _():
                wait_rows(recv_sems.at[0], pieces * others)

    for distance in (1, -1):

        @pl.when(near(distance))
        def _():
            wait_rows(recv_sems.at[2 - distance], OWN)

    primal_2 = primal_update(primal_1, adjoint(window_next))
    terms_b[...] = forward(2.0 * primal_2 - primal_1)
    for distance, when in ((1, far(1)), (-1, far(-1)), (1, near(1)), (-1, near(-1)), (0, exists(0))):

        @pl.when(when)
        def _():
            to_owners(distance, copy_b)

    primals[0] = primal_1
    primals[1] = primal_2
    results = [
        pltpu.make_async_copy(primals, primal_out, out_sems.at[0]),
        pltpu.make_async_copy(window_next.at[:, 1], dual_out.at[0], out_sems.at[1]),
    ]
    for copy in results:
        copy.start()


    @pl.when(is_owner)
    def _():
        own = pl.ds(pl.multiple_of(mine * 3 * PIECE + PIECE, 8), PIECE)
        parts_b[pl.ds(pl.multiple_of(group * 3 * PIECE + PIECE, 8), PIECE)] = terms_b[own]
        def summed(first):
            return sum(
                parts_b[pl.ds(pl.multiple_of((index * 3 + first) * PIECE, PIECE), PIECE)] for index in range(8)
            )

        wait_rows(sums_recv.at[1, 2], 7)
        for distance in (1, -1):

            @pl.when(near(distance))
            def _():
                wait_rows(sums_recv.at[1, distance + 2], 8)

        near_block = jnp.where(time == LAST, 0, 2)
        early = summed(1) + summed(near_block)
        for distance in (1, -1):

            @pl.when(far(distance))
            def _():
                wait_rows(sums_recv.at[1, distance + 2], 8)

        image = early + summed(2 - near_block)
        piece_b[...] = jnp.maximum(piece_a[1] + STEP * (window_rhs[1] - image), 0.0)
        for offset in (3, 5, 1, 7, 4, 2, 6):
            from_owner(piece_b, dual_out.at[1, mine], offset, 0, 2).start()
        own_copy = pltpu.make_async_copy(piece_b, dual_out.at[1, mine], out_sems.at[2])
        own_copy.start()
        wait_rows(recv_sems.at[2], OWN - 1)
        own_copy.wait()

    @pl.when(jnp.logical_not(is_owner))
    def _():
        wait_rows(recv_sems.at[2], OWN)

    for copy in results:
        copy.wait()

    for distance in (1, -1):
        for when, copies in dual_copies(distance):

            @pl.when(when)
            def _():
                for copy in copies:
                    copy.wait_send()

    for distance in (1, -1):

        @pl.when(on_core & exists(distance))
        def _():
            pass_on(distance).wait_send()

    two_steps = ((2, time == LAST - 1), (-2, time == NEXT + 1))

    @pl.when(is_owner)
    def _():
        for distance in (1, -1):

            @pl.when(far(distance))
            def _():
                rhs_copy(distance).wait_send()

            @pl.when(near(distance))
            def _():
                wait_rows(send_sems.at[2 + distance], 8)

        wait_sums_a(sums_sent, two_steps, OWN, OWN - 1)
        wait_sums_b(sums_sent, OWN, OWN - 1)
        for pieces, when in ((2, edge), (1, jnp.logical_not(edge))):

            @pl.when(when)
            def _():
                wait_rows(send_sems.at[0], 7 * pieces)

        wait_rows(send_sems.at[2], 7)

    @pl.when(jnp.logical_not(is_owner))
    def _():
        wait_sums_a(sums_sent, two_steps, OWN, OWN)
        wait_sums_b(sums_sent, OWN, OWN)


def means(primals_ref, duals_ref, primal_out, dual_out, primal_mean_out, dual_mean_out):
    for iterates, last, mean in ((primals_ref, primal_out, primal_mean_out), (duals_ref, dual_out, dual_mean_out)):
        last[...] = iterates[1]
        mean[...] = (iterates[0] + iterates[1]) / ITERS


def body(
    x_start,
    y_start,
    cost,
    rhs,
    tiles,
    tile_rows,
    tile_cols,
    tile_count,
    var_class,
    lower_table,
    upper_table,
):
    vmem = pl.BlockSpec(memory_space=pltpu.VMEM)
    primals, duals = pl.pallas_call(
        kernel,
        name="pdhg",
        out_shape=(
            jax.ShapeDtypeStruct((ITERS, CB, TILE), F32),
            jax.ShapeDtypeStruct((ITERS, OWN, PIECE, TILE), F32),
        ),
        in_specs=[pl.BlockSpec(memory_space=pltpu.HBM)] * 12,
        out_specs=(pl.BlockSpec(memory_space=pl.ANY),) * 2,
        scratch_shapes=[
            pltpu.VMEM((CB, TILE), F32),
            pltpu.VMEM((OWN, PIECE, TILE), F32),
            pltpu.VMEM((CB, TILE), F32),
            pltpu.VMEM((OWN, PIECE, TILE), F32),
            pltpu.SMEM((NT,), jnp.int32),
            pltpu.SMEM((1,), jnp.int32),
            pltpu.VMEM((1, NT), jnp.int32),
            pltpu.VMEM((1, NT), jnp.int32),
            pltpu.VMEM((CB, TILE), jnp.int32),
            pltpu.VMEM((1, 8), F32),
            pltpu.VMEM((1, 8), F32),
            pltpu.VMEM((NT, TILE, TILE), F32),
            pltpu.VMEM((NT, TILE, TILE), F32),
            pltpu.VMEM((CB, TILE, TILE), F32),
            pltpu.VMEM((max(HALVED, 1) * TILE, 2 * TILE), BF16),
            pltpu.VMEM((2 * CB, max(AM, 1) * TILE), BF16),
            pltpu.VMEM((max(FM, 1), CB, TILE), F32),
            pltpu.VMEM((WIN, 16 * (NT - FM) + 2 * FM), BF16),
            pltpu.VMEM((CB, 16 * (NT - AM)), BF16),
            pltpu.VMEM((8 * NT, TILE), F32),
            pltpu.VMEM((2 * WIN, NT), BF16),
            pltpu.VMEM((max(AM, 1), 2 * WIN), BF16),
            pltpu.VMEM((OWN, 3, PIECE, TILE), F32),
            pltpu.VMEM((3, PIECE, TILE), F32),
            pltpu.VMEM((OWN, 3, PIECE, TILE), F32),
            pltpu.VMEM((WIN, TILE), F32),
            pltpu.VMEM((WIN, TILE), F32),
            pltpu.VMEM((8 * SLOT_ROWS, TILE), F32),
            pltpu.VMEM((8 * 3 * PIECE, TILE), F32),
            pltpu.VMEM((3, PIECE, TILE), F32),
            pltpu.VMEM((PIECE, TILE), F32),
            pltpu.VMEM((ITERS, CB, TILE), F32),
            pltpu.SemaphoreType.DMA((NT // CHUNK,)),
            pltpu.SemaphoreType.DMA((3,)),
            pltpu.SemaphoreType.DMA((11,)),
            pltpu.SemaphoreType.DMA((8,)),
            pltpu.SemaphoreType.DMA((8,)),
            pltpu.SemaphoreType.DMA((2, 5)),
            pltpu.SemaphoreType.DMA((2, 5)),
            pltpu.SemaphoreType.DMA((4,)),
            pltpu.SemaphoreType.DMA((4,)),
        ],
        compiler_params=pltpu.CompilerParams(
            collective_id=0, has_side_effects=True, vmem_limit_bytes=60 * 1024 * 1024
        ),
    )(
        x_start,
        y_start.reshape(OWN, PIECE, TILE),
        cost,
        rhs.reshape(OWN, PIECE, TILE),
        tiles,
        tile_cols,
        tile_count,
        tile_rows.reshape(1, NT),
        tile_cols.reshape(1, NT),
        var_class,
        lower_table.reshape(1, 8),
        upper_table.reshape(1, 8),
    )
    columns = jax.ShapeDtypeStruct((CB, TILE), F32)
    rows = jax.ShapeDtypeStruct((RB, TILE), F32)
    return pl.pallas_call(
        means,
        name="means",
        out_shape=(columns, rows, columns, rows),
        in_specs=[vmem, vmem],
        out_specs=(vmem, vmem, vmem, vmem),
    )(primals, duals.reshape(ITERS, RB, TILE))


def solution(mesh):
    return jax.shard_map(
        body,
        mesh=mesh,
        in_specs=(
            P(("grp", "tm"), None),
            P("tm", None),
            P(("grp", "tm"), None),
            P("tm", None),
            P(("grp", "tm"), None, None),
            P(("grp", "tm")),
            P(("grp", "tm")),
            P(("grp", "tm")),
            P(("grp", "tm"), None),
            P(),
            P(),
        ),
        out_specs=(P(("grp", "tm"), None), P("tm", None), P(("grp", "tm"), None), P("tm", None)),
        check_vma=False,
    )
```

```python
import jax
import jax.numpy as jnp
from jax import lax
from jax.experimental import pallas as pl
from jax.experimental.pallas import tpu as pltpu
from jax.sharding import PartitionSpec as P

ITERS = 2
STEP = 0.6
MESH = pl.DeviceIdType.MESH
F32 = jnp.float32
BF16 = jnp.bfloat16

NT = 64
TILE = 128
CB = 16
RB = 32
OWN = 2
PIECE = RB // OWN
WIN = 3 * RB
CHUNK = 8
AM = 48
FM = 16
HALVED = max(AM, FM)

LAST, NEXT = 15, 16
SLOT_ROWS = 6 * PIECE


def split(value):
    high = value.astype(BF16)
    return high, (value - high.astype(F32)).astype(BF16)


def kernel(
    x_hbm,
    y_hbm,
    cost_hbm,
    rhs_hbm,
    tiles_hbm,
    cols_hbm,
    count_hbm,
    rowv_hbm,
    colv_hbm,
    class_hbm,
    lower_hbm,
    upper_hbm,
    primal_out,
    dual_out,
    x_ref,
    y_ref,
    cost_ref,
    rhs_ref,
    cols_ref,
    count_ref,
    rowv_ref,
    colv_ref,
    class_ref,
    lower_ref,
    upper_ref,
    staged,
    turned,
    factors,
    weights,
    placed,
    product,
    select_f,
    select_a,
    partial,
    pick,
    pick_last,
    window_y,
    window_rhs,
    window_next,
    terms_a,
    terms_b,
    parts_a,
    parts_b,
    piece_a,
    piece_b,
    primals,
    load_sem,
    out_sems,
    input_sems,
    dual_sems,
    halo_sems,
    sums_sent,
    sums_recv,
    send_sems,
    recv_sems,
):
    group = lax.axis_index("grp")
    time = lax.axis_index("tm")
    place = group // 2
    core = lax.rem(group, 2)
    on_core = core == 1
    is_owner = on_core & ((place == 1) | (place == 2))
    mine = place // 2

    def at(distance):
        return time + distance

    def exists(distance):
        there = time + distance
        return (there >= 0) & (there < 32)

    def number(distances):
        return sum(jnp.where(exists(distance), 1, 0) for distance in distances)

    def owner(offset):
        return lax.rem(mine + offset, OWN)

    def owner_group(offset):
        return 2 * owner(offset) + 3

    def far(distance):
        return (time == LAST) if distance > 0 else (time == NEXT)

    def near(distance):
        return exists(distance) & jnp.logical_not(far(distance))

    edge = (time == LAST) | (time == NEXT)
    at_end = (place == 0) | (place == 3)

    def both(distance):
        return edge if distance == 0 else far(distance)

    window_rhs[...] = jnp.zeros_like(window_rhs)

    @pl.when(jnp.logical_not(edge))
    def _():
        parts_a[...] = jnp.zeros_like(parts_a)

    @pl.when((time == 0) | (time == 31))
    def _():
        parts_b[...] = jnp.zeros_like(parts_b)
        window_y[...] = jnp.zeros_like(window_y)
        window_next[...] = jnp.zeros_like(window_next)

    barrier = pltpu.get_barrier_semaphore()

    def greet(target_group, target_time):
        pl.semaphore_signal(
            barrier, inc=1, device_id=(target_group, target_time), device_id_type=MESH
        )

    def greet_all(distance):
        for offset in range(7, -1, -1):
            if distance or offset:
                greet(lax.rem(group + offset, 8), at(distance))

    source_place = jnp.where(place >= 2, 0, 3)
    left = jnp.where(place == 3, 0, 2)

    @pl.when(is_owner)
    def _():
        for distance, when in ((2, time == LAST), (-2, time == NEXT), (1, exists(1)), (-1, exists(-1))):

            @pl.when(when)
            def _():
                greet_all(distance)

        greet_all(0)

    @pl.when(jnp.logical_not(is_owner))
    def _():
        for distance in (1, -1):

            @pl.when(on_core & far(distance))
            def _():
                greet(2 * source_place + 1, at(distance))

            @pl.when(on_core & near(distance))
            def _():
                greet(group, at(distance))

            @pl.when(near(distance))
            def _():
                for offset in range(OWN):
                    greet(owner_group(offset), at(distance))

        for offset in range(OWN):
            greet(owner_group(offset), time)

        @pl.when(jnp.logical_not(on_core) & at_end)
        def _():
            greet(group + 1, time)

    inputs = []
    for index, (source, target) in enumerate(
        (
            (y_hbm, y_ref),
            (rhs_hbm, rhs_ref),
            (x_hbm, x_ref),
            (cost_hbm, cost_ref),
            (class_hbm, class_ref),
            (rowv_hbm, rowv_ref),
            (colv_hbm, colv_ref),
            (count_hbm, count_ref),
            (lower_hbm, lower_ref),
            (upper_hbm, upper_ref),
            (cols_hbm, cols_ref),
        )
    ):
        copy = pltpu.make_async_copy(source, target, input_sems.at[index])
        copy.start()
        inputs.append(copy)
    loads = []
    for chunk in range(NT // CHUNK):
        span = pl.ds(chunk * CHUNK, CHUNK)
        load = pltpu.make_async_copy(tiles_hbm.at[span], staged.at[span], load_sem.at[chunk])
        load.start()
        loads.append(load)
    for copy in inputs:
        copy.wait()

    of_owner = 7
    for distance in (1, -1):
        of_owner = of_owner + jnp.where(near(distance), 8, 0)
        of_owner = of_owner + jnp.where(far(distance), OWN, 0)
    two_steps = jnp.where((time == LAST - 1) | (time == NEXT + 1), OWN, 0)
    of_other = OWN * number((1, 0, -1))
    of_sender = of_other + number((1, -1)) + 1
    peers = jnp.where(is_owner, of_owner, jnp.where(on_core, of_sender, of_other))
    pl.semaphore_wait(barrier, peers + two_steps)

    def dual_copies(distance):
        slot = 1 - distance

        def copy(target, number):
            return pltpu.make_async_remote_copy(
                src_ref=y_ref,
                dst_ref=window_y.at[:, slot],
                send_sem=dual_sems.at[slot // 2 * 4 + number],
                recv_sem=halo_sems.at[slot],
                device_id=(2 * target + 1, at(distance)),
                device_id_type=MESH,
            )

        return [
            (on_core & far(distance) & at_end, [copy(left, 0), copy(left + 1, 1)]),
            (on_core & near(distance), [copy(place, 2)]),
        ]

    def pass_on(distance):
        slot = 1 + distance
        return pltpu.make_async_remote_copy(
            src_ref=window_y.at[:, slot],
            dst_ref=window_y.at[:, slot],
            send_sem=dual_sems.at[slot // 2 * 4 + 3],
            recv_sem=halo_sems.at[slot],
            device_id=(group - 1, time),
            device_id_type=MESH,
        )

    def rhs_copy(distance):
        slot = 1 - distance
        return pltpu.make_async_remote_copy(
            src_ref=rhs_ref.at[mine],
            dst_ref=window_rhs.at[slot],
            send_sem=halo_sems.at[slot + 4],
            recv_sem=halo_sems.at[slot + 1],
            device_id=(group, at(distance)),
            device_id_type=MESH,
        )

    for distance in (1, -1):
        for when, copies in dual_copies(distance):

            @pl.when(when)
            def _():
                for copy in copies:
                    copy.start()

    @pl.when(is_owner)
    def _():
        for distance in (1, -1):

            @pl.when(far(distance))
            def _():
                rhs_copy(distance).start()

    window_y[:, 1] = y_ref[...]
    window_rhs[1] = rhs_ref[mine]

    for chunk in range(NT // CHUNK):
        loads[chunk].wait()

        def turn(slot, carry):
            turned[slot] = staged[slot].T
            return carry

        if chunk * CHUNK < NT - FM:
            lax.fori_loop(chunk * CHUNK, (chunk + 1) * CHUNK, turn, 0, unroll=4)

        def halve(slot, carry):
            high, low = split(staged[slot])
            base = pl.multiple_of((slot - (NT - HALVED)) * TILE, TILE)
            weights[pl.ds(base, TILE), 0:TILE] = high
            weights[pl.ds(base, TILE), TILE : 2 * TILE] = low
            return carry

        if chunk * CHUNK >= NT - HALVED:
            lax.fori_loop(chunk * CHUNK, (chunk + 1) * CHUNK, halve, 0, unroll=4)

    var_class = class_ref[...]
    lower = jnp.zeros((CB, TILE), F32)
    upper = jnp.zeros((CB, TILE), F32)
    for class_id in range(lower_ref.shape[1]):
        lower = jnp.where(var_class == class_id, lower_ref[:, class_id : class_id + 1], lower)
        upper = jnp.where(var_class == class_id, upper_ref[:, class_id : class_id + 1], upper)

    first_row = (time - 1) * RB
    first_col = (group * 32 + time) * CB
    slot_id = lax.broadcasted_iota(jnp.int32, (WIN, NT), 1)
    window_id = lax.broadcasted_iota(jnp.int32, (WIN, NT), 0)
    owner_id = window_id // (3 * PIECE)
    block_id = window_id // PIECE - 3 * owner_id
    row_id = block_id * RB + owner_id * PIECE + lax.rem(window_id, PIECE)
    scatter = ((rowv_ref[...] - first_row) == row_id) & (slot_id < count_ref[0])
    gather = ((colv_ref[...] - first_col) == window_id[:CB]) & (slot_id[:CB] < count_ref[0])
    scatter = jnp.where(scatter, 1.0, 0.0)
    chosen = jnp.concatenate([scatter, jnp.where(gather, 1.0, 0.0)], axis=0)
    pick[...] = jnp.concatenate([scatter, scatter], axis=0).astype(BF16)
    if AM:
        last = scatter.T[NT - AM :]
        pick_last[...] = jnp.concatenate([last, last], axis=1).astype(BF16)
    chosen = chosen.astype(BF16)

    def spread(alone):
        width = 8 * (NT - alone) + alone
        lane = lax.broadcasted_iota(jnp.int32, (NT, width), 1)
        owner_slot = jnp.where(lane < 8 * (NT - alone), lane // 8, lane - 7 * (NT - alone))
        hit = owner_slot == lax.broadcasted_iota(jnp.int32, (NT, width), 0)
        return jnp.where(hit, 1.0, 0.0).astype(BF16)

    def twice(value):
        value = value.astype(BF16)
        return jnp.concatenate([value, value], axis=1)

    select_f[...] = twice(jnp.dot(chosen[:WIN], spread(FM), preferred_element_type=F32))
    select_a[...] = twice(
        jnp.dot(chosen[WIN:], spread(0)[:, : 8 * (NT - AM)], preferred_element_type=F32)
    )

    def add_up(select, values):
        high, low = split(values)
        return jnp.dot(select, jnp.concatenate([high, low], axis=0), preferred_element_type=F32)

    def fold(value):
        return jnp.sum(value.reshape(TILE // 8, 8, TILE), axis=0)

    sub_id = lax.broadcasted_iota(jnp.int32, (CB, TILE), 0)

    def adjoint(field):
        field = field[...].reshape(WIN, TILE)
        high, low = split(field.T)
        columns = jnp.dot(
            jnp.concatenate([high, low], axis=1), pick[...], preferred_element_type=F32
        )
        if AM:
            high, low = split(field)
            rows = lax.dot_general(
                pick_last[...],
                jnp.concatenate([high, low], axis=0),
                (((1,), (0,)), ((), ())),
                preferred_element_type=F32,
            )
            for index in range(AM):
                here = sub_id == cols_ref[NT - AM + index] - first_col
                value = rows[index : index + 1]
                high = value.astype(BF16).astype(F32)
                span = slice(index * TILE, (index + 1) * TILE)
                placed[0:CB, span] = jnp.where(here, high, 0.0).astype(BF16)
                placed[CB : 2 * CB, span] = jnp.where(here, value - high, 0.0).astype(BF16)
            total = jnp.dot(placed[...], weights[(HALVED - AM) * TILE :], preferred_element_type=F32)
            total = total[:CB] + total[CB:]
            total = total[:, :TILE] + total[:, TILE:]
        for slot in range(NT - AM):
            factor = jnp.broadcast_to(columns[:, slot : slot + 1], (TILE, TILE))
            partial[8 * slot : 8 * slot + 8] = fold(staged[slot] * factor)
        rest = add_up(select_a[...], partial[0 : 8 * (NT - AM)])
        return total + rest if AM else rest

    def forward(field):
        if FM:
            high, low = split(field)
            halves = jnp.concatenate([high, low], axis=0)
            result = lax.dot_general(
                jnp.concatenate([halves, halves], axis=1),
                weights[(HALVED - FM) * TILE :],
                (((1,), (1,)), ((), ())),
                preferred_element_type=F32,
            )
            for index in range(FM):
                span = slice(index * TILE, (index + 1) * TILE)
                product[index] = result[:CB, span] + result[CB:, span]
        columns = field.T
        for block in range(CB):
            factors[block] = jnp.broadcast_to(columns[:, block : block + 1], (TILE, TILE))

        def product_of(slot, carry):
            col = jnp.clip(cols_ref[slot] - first_col, 0, CB - 1)
            partial[pl.ds(pl.multiple_of(8 * slot, 8), 8)] = fold(turned[slot] * factors[col])
            return carry

        lax.fori_loop(0, NT - FM, product_of, 0, unroll=16)
        for index in range(FM):
            col = jnp.clip(cols_ref[NT - FM + index] - first_col, 0, CB - 1)
            row = 8 * (NT - FM) + index
            partial[row : row + 1] = product[index, pl.ds(col, 1), :]
        return add_up(select_f[...], partial[0 : 8 * (NT - FM) + FM])

    def primal_update(primal, adjoint_part):
        moved = primal - STEP * (cost_ref[...] - adjoint_part)
        return jnp.minimum(jnp.maximum(moved, lower), upper)

    def to_owner(source, target, distance, offset, sems):
        return pltpu.make_async_remote_copy(
            src_ref=source,
            dst_ref=target,
            send_sem=sums_sent.at[sems, distance + 2],
            recv_sem=sums_recv.at[sems, 2 - distance],
            device_id=(owner_group(offset), at(distance)),
            device_id_type=MESH,
        )

    def from_owner(source, target, offset, distance, semaphore):
        return pltpu.make_async_remote_copy(
            src_ref=source,
            dst_ref=target,
            send_sem=send_sems.at[semaphore],
            recv_sem=recv_sems.at[semaphore],
            device_id=(lax.rem(group + offset, 8), at(distance)),
            device_id_type=MESH,
        )

    def rows_of(ref, first, pieces):
        return ref.at[pl.ds(pl.multiple_of(first, PIECE), pieces * PIECE)]

    def copy_a(distance, offset, pieces):
        block = jnp.where(time == NEXT, 0, 1) if distance == 0 else 2 if distance > 0 else 0
        if pieces == 2:
            block = jnp.where(time == NEXT, 0, 1)
        region = {
            0: 0,
            1: jnp.where(time + 1 == NEXT, 2, 4),
            -1: jnp.where(time - 1 == NEXT, 4, 2),
            2: 5,
            -2: 5,
        }[distance]
        if distance == 0 and pieces == 1:
            block = 1
        source = rows_of(terms_a, (owner(offset) * 3 + block) * PIECE, pieces)
        target = rows_of(parts_a, group * SLOT_ROWS + region * PIECE, pieces)
        return to_owner(source, target, distance, offset, 0)

    def copy_b(distance, offset):
        source = rows_of(terms_b, (owner(offset) * 3 + 1 + distance) * PIECE, 1)
        target = rows_of(parts_b, (group * 3 + 1 - distance) * PIECE, 1)
        return to_owner(source, target, distance, offset, 1)

    def to_owners(distance, copy):
        for offset in (1, 0):
            if distance or offset:
                copy(distance, offset).start()
            else:

                @pl.when(jnp.logical_not(is_owner))
                def _():
                    copy(distance, offset).start()

    def steps_a():
        for distance in (1, -1, 0):
            yield distance, exists(distance) & both(distance), 2
        for distance in (1, -1, 0):
            yield distance, exists(distance) & jnp.logical_not(both(distance)), 1

    def wait_rows(semaphore, pieces):
        ref = parts_a.at[0 : pieces * PIECE]
        pltpu.make_async_copy(ref, ref, semaphore).wait()

    def wait_sums_a(semaphores, two_steps, copies, own):
        for distance, when, pieces in steps_a():

            @pl.when(when)
            def _():
                wait_rows(semaphores.at[0, distance + 2], pieces * (copies if distance else own))

        for distance, when in two_steps:

            @pl.when(when)
            def _():
                wait_rows(semaphores.at[0, distance + 2], copies)

    def wait_sums_b(semaphores, copies, own):
        for distance in (1, -1, 0):

            @pl.when(exists(distance))
            def _():
                wait_rows(semaphores.at[1, distance + 2], copies if distance else own)

    for distance, when in ((1, near(1)), (-1, near(-1)), (1, far(1)), (-1, far(-1))):

        @pl.when(when)
        def _():
            dual_in = window_y.at[:, 1 + distance]
            pltpu.make_async_copy(dual_in, dual_in, halo_sems.at[1 + distance]).wait()

            @pl.when(on_core)
            def _():
                pass_on(distance).start()

    primal_0 = x_ref[...]
    primal_1 = primal_update(primal_0, adjoint(window_y))
    terms_a[...] = forward(2.0 * primal_1 - primal_0)
    for distance, when in ((2, time == LAST - 1), (-2, time == NEXT + 1)):

        @pl.when(when)
        def _():
            to_owners(distance, lambda distance, offset: copy_a(distance, offset, 1))

    for distance, when, pieces in steps_a():

        @pl.when(when)
        def _():
            to_owners(distance, lambda distance, offset: copy_a(distance, offset, pieces))

    @pl.when(is_owner)
    def _():
        for pieces, when in ((2, edge), (1, jnp.logical_not(edge))):

            @pl.when(when)
            def _():
                block = jnp.where(time == NEXT, 0, 1) if pieces == 2 else 1
                source = pl.ds(pl.multiple_of((mine * 3 + block) * PIECE, 8), pieces * PIECE)
                target = pl.ds(pl.multiple_of(group * SLOT_ROWS, 8), pieces * PIECE)
                parts_a[target] = terms_a[source]

        def summed(ref, stride, first):
            return sum(
                ref[pl.ds(pl.multiple_of((index * stride + first) * PIECE, PIECE), PIECE)] for index in range(8)
            )

        for distance, when, pieces in steps_a():

            @pl.when(when & jnp.logical_not(far(distance) if distance else False))
            def _():
                wait_rows(sums_recv.at[0, distance + 2], pieces * (8 if distance else 7))

        early = [summed(parts_a, 6, index) for index in (0, 1, 4)]
        for distance in (1, -1):

            @pl.when(far(distance))
            def _():
                rhs_in = window_rhs.at[1 + distance]
                pltpu.make_async_copy(rhs_in, rhs_in, halo_sems.at[2 + distance]).wait()
                wait_rows(sums_recv.at[0, distance + 2], 2 * 8)

        for distance, when in ((2, time == LAST), (-2, time == NEXT)):

            @pl.when(when)
            def _():
                wait_rows(sums_recv.at[0, distance + 2], 8)

        step = [early[0], early[1], summed(parts_a, 6, 2), summed(parts_a, 6, 3), early[2], summed(parts_a, 6, 5)]
        low = step[0] + step[2]
        high = step[1] + step[3]
        upper_side = time == NEXT
        first = jnp.where(upper_side, high, low) + step[4]
        second = jnp.where(upper_side, low, high) + step[5]
        for block in range(3):
            image = first if block == 1 else second
            piece_a[block] = jnp.maximum(window_y[mine, block] + STEP * (window_rhs[block] - image), 0.0)
        @pl.when(edge)
        def _():
            span = pl.ds(jnp.where(time == NEXT, 0, 1), 2)
            for offset in (3, 5, 1, 7, 4, 2, 6):
                from_owner(piece_a.at[span], window_next.at[mine, span], offset, 0, 0).start()
            window_next[mine, span] = piece_a[span]

        @pl.when(jnp.logical_not(edge))
        def _():
            for offset in (3, 5, 1, 7, 4, 2, 6):
                from_owner(piece_a.at[1], window_next.at[mine, 1], offset, 0, 0).start()
            window_next[mine, 1] = piece_a[1]

        for distance in (1, -1):

            @pl.when(near(distance))
            def _():
                for offset in range(7, -1, -1):
                    from_owner(
                        piece_a.at[1], window_next.at[mine, 1 - distance], offset, distance, 2 + distance
                    ).start()

    for owned, others in ((is_owner, OWN - 1), (jnp.logical_not(is_owner), OWN)):
        for pieces, when in ((2, edge), (1, jnp.logical_not(edge))):

            @pl.when(owned & when)
            def _():
                wait_rows(recv_sems.at[0], pieces * others)

    for distance in (1, -1):

        @pl.when(near(distance))
        def _():
            wait_rows(recv_sems.at[2 - distance], OWN)

    primal_2 = primal_update(primal_1, adjoint(window_next))
    terms_b[...] = forward(2.0 * primal_2 - primal_1)
    for distance, when in ((1, far(1)), (-1, far(-1)), (1, near(1)), (-1, near(-1)), (0, exists(0))):

        @pl.when(when)
        def _():
            to_owners(distance, copy_b)

    primals[0] = primal_1
    primals[1] = primal_2
    results = [
        pltpu.make_async_copy(primals, primal_out, out_sems.at[0]),
        pltpu.make_async_copy(window_next.at[:, 1], dual_out.at[0], out_sems.at[1]),
    ]
    for copy in results:
        copy.start()


    @pl.when(is_owner)
    def _():
        own = pl.ds(pl.multiple_of(mine * 3 * PIECE + PIECE, 8), PIECE)
        parts_b[pl.ds(pl.multiple_of(group * 3 * PIECE + PIECE, 8), PIECE)] = terms_b[own]
        def summed(first):
            return sum(
                parts_b[pl.ds(pl.multiple_of((index * 3 + first) * PIECE, PIECE), PIECE)] for index in range(8)
            )

        wait_rows(sums_recv.at[1, 2], 7)
        for distance in (1, -1):

            @pl.when(near(distance))
            def _():
                wait_rows(sums_recv.at[1, distance + 2], 8)

        near_block = jnp.where(time == LAST, 0, 2)
        early = summed(1) + summed(near_block)
        for distance in (1, -1):

            @pl.when(far(distance))
            def _():
                wait_rows(sums_recv.at[1, distance + 2], 8)

        image = early + summed(2 - near_block)
        piece_b[...] = jnp.maximum(piece_a[1] + STEP * (window_rhs[1] - image), 0.0)
        for offset in (3, 5, 1, 7, 4, 2, 6):
            from_owner(piece_b, dual_out.at[1, mine], offset, 0, 2).start()
        own_copy = pltpu.make_async_copy(piece_b, dual_out.at[1, mine], out_sems.at[2])
        own_copy.start()
        wait_rows(recv_sems.at[2], OWN - 1)
        own_copy.wait()

    @pl.when(jnp.logical_not(is_owner))
    def _():
        wait_rows(recv_sems.at[2], OWN)

    for copy in results:
        copy.wait()

    for distance in (1, -1):
        for when, copies in dual_copies(distance):

            @pl.when(when)
            def _():
                for copy in copies:
                    copy.wait_send()

    for distance in (1, -1):

        @pl.when(on_core & exists(distance))
        def _():
            pass_on(distance).wait_send()

    two_steps = ((2, time == LAST - 1), (-2, time == NEXT + 1))

    @pl.when(is_owner)
    def _():
        for distance in (1, -1):

            @pl.when(far(distance))
            def _():
                rhs_copy(distance).wait_send()

            @pl.when(near(distance))
            def _():
                wait_rows(send_sems.at[2 + distance], 8)

        wait_sums_a(sums_sent, two_steps, OWN, OWN - 1)
        wait_sums_b(sums_sent, OWN, OWN - 1)
        for pieces, when in ((2, edge), (1, jnp.logical_not(edge))):

            @pl.when(when)
            def _():
                wait_rows(send_sems.at[0], 7 * pieces)

        wait_rows(send_sems.at[2], 7)

    @pl.when(jnp.logical_not(is_owner))
    def _():
        wait_sums_a(sums_sent, two_steps, OWN, OWN)
        wait_sums_b(sums_sent, OWN, OWN)


def means(primals_ref, duals_ref, primal_out, dual_out, primal_mean_out, dual_mean_out):
    for iterates, last, mean in ((primals_ref, primal_out, primal_mean_out), (duals_ref, dual_out, dual_mean_out)):
        last[...] = iterates[1]
        mean[...] = (iterates[0] + iterates[1]) / ITERS


def body(
    x_start,
    y_start,
    cost,
    rhs,
    tiles,
    tile_rows,
    tile_cols,
    tile_count,
    var_class,
    lower_table,
    upper_table,
):
    vmem = pl.BlockSpec(memory_space=pltpu.VMEM)
    primals, duals = pl.pallas_call(
        kernel,
        name="pdhg",
        out_shape=(
            jax.ShapeDtypeStruct((ITERS, CB, TILE), F32),
            jax.ShapeDtypeStruct((ITERS, OWN, PIECE, TILE), F32),
        ),
        in_specs=[pl.BlockSpec(memory_space=pltpu.HBM)] * 12,
        out_specs=(pl.BlockSpec(memory_space=pl.ANY),) * 2,
        scratch_shapes=[
            pltpu.VMEM((CB, TILE), F32),
            pltpu.VMEM((OWN, PIECE, TILE), F32),
            pltpu.VMEM((CB, TILE), F32),
            pltpu.VMEM((OWN, PIECE, TILE), F32),
            pltpu.SMEM((NT,), jnp.int32),
            pltpu.SMEM((1,), jnp.int32),
            pltpu.VMEM((1, NT), jnp.int32),
            pltpu.VMEM((1, NT), jnp.int32),
            pltpu.VMEM((CB, TILE), jnp.int32),
            pltpu.VMEM((1, 8), F32),
            pltpu.VMEM((1, 8), F32),
            pltpu.VMEM((NT, TILE, TILE), F32),
            pltpu.VMEM((NT, TILE, TILE), F32),
            pltpu.VMEM((CB, TILE, TILE), F32),
            pltpu.VMEM((max(HALVED, 1) * TILE, 2 * TILE), BF16),
            pltpu.VMEM((2 * CB, max(AM, 1) * TILE), BF16),
            pltpu.VMEM((max(FM, 1), CB, TILE), F32),
            pltpu.VMEM((WIN, 16 * (NT - FM) + 2 * FM), BF16),
            pltpu.VMEM((CB, 16 * (NT - AM)), BF16),
            pltpu.VMEM((8 * NT, TILE), F32),
            pltpu.VMEM((2 * WIN, NT), BF16),
            pltpu.VMEM((max(AM, 1), 2 * WIN), BF16),
            pltpu.VMEM((OWN, 3, PIECE, TILE), F32),
            pltpu.VMEM((3, PIECE, TILE), F32),
            pltpu.VMEM((OWN, 3, PIECE, TILE), F32),
            pltpu.VMEM((WIN, TILE), F32),
            pltpu.VMEM((WIN, TILE), F32),
            pltpu.VMEM((8 * SLOT_ROWS, TILE), F32),
            pltpu.VMEM((8 * 3 * PIECE, TILE), F32),
            pltpu.VMEM((3, PIECE, TILE), F32),
            pltpu.VMEM((PIECE, TILE), F32),
            pltpu.VMEM((ITERS, CB, TILE), F32),
            pltpu.SemaphoreType.DMA((NT // CHUNK,)),
            pltpu.SemaphoreType.DMA((3,)),
            pltpu.SemaphoreType.DMA((11,)),
            pltpu.SemaphoreType.DMA((8,)),
            pltpu.SemaphoreType.DMA((8,)),
            pltpu.SemaphoreType.DMA((2, 5)),
            pltpu.SemaphoreType.DMA((2, 5)),
            pltpu.SemaphoreType.DMA((4,)),
            pltpu.SemaphoreType.DMA((4,)),
        ],
        compiler_params=pltpu.CompilerParams(
            collective_id=0, has_side_effects=True, vmem_limit_bytes=60 * 1024 * 1024
        ),
    )(
        x_start,
        y_start.reshape(OWN, PIECE, TILE),
        cost,
        rhs.reshape(OWN, PIECE, TILE),
        tiles,
        tile_cols,
        tile_count,
        tile_rows.reshape(1, NT),
        tile_cols.reshape(1, NT),
        var_class,
        lower_table.reshape(1, 8),
        upper_table.reshape(1, 8),
    )
    columns = jax.ShapeDtypeStruct((CB, TILE), F32)
    rows = jax.ShapeDtypeStruct((RB, TILE), F32)
    return pl.pallas_call(
        means,
        name="means",
        out_shape=(columns, rows, columns, rows),
        in_specs=[vmem, vmem],
        out_specs=(vmem, vmem, vmem, vmem),
    )(primals, duals.reshape(ITERS, RB, TILE))


def solution(mesh):
    return jax.shard_map(
        body,
        mesh=mesh,
        in_specs=(
            P(("grp", "tm"), None),
            P("tm", None),
            P(("grp", "tm"), None),
            P("tm", None),
            P(("grp", "tm"), None, None),
            P(("grp", "tm")),
            P(("grp", "tm")),
            P(("grp", "tm")),
            P(("grp", "tm"), None),
            P(),
            P(),
        ),
        out_specs=(P(("grp", "tm"), None), P("tm", None), P(("grp", "tm"), None), P("tm", None)),
        check_vma=False,
    )
```
